32 devices in a mesh: pole: 2 (over x), row: 4 (over y, core), col: 4 (over z).
Axes of the slice: x: 2, y: 2, z: 4, core: 2. Of those that a mesh axis runs over, the one named last changes fastest.
Arguments:
- inverse_top: bfloat16 [4, 1, 4, 256, 1, 4, 256], P('pole', None, 'row', None, None, 'col'), parts along dimension 0, may hold values from -0.25 to 0.25
- factor: bfloat16 [4, 4, 1, 4, 128, 256], P('col', 'pole', None, 'row'), parts along dimension 1, may hold values from -1.5 to 1.5
- diag_inverse: float32 [4, 4, 256, 256], P('col', 'pole'), parts along dimension 1, may hold values from -12 to 12
- row_lists: int32 [4, 4, 128], replicated, may hold values from 0 to 255, as said below
Outputs:
- inverse_block: float32 [4, 4, 1, 4, 128, 256], P('col', 'pole', None, 'row'), parts along dimension 1
- diagonal_block: float32 [4, 4, 256, 256], P('col', 'pole'), parts along dimension 1
The draws below stay inside these ranges and needn't reach their ends.
There are 2 independent parts, one for each index of `pole`. The reference program is written for one: setup_inputs(seed, part) draws one part's arguments, and reference() takes and returns one part's arrays. A program takes and returns all parts, laid end to end along the dimension named above; an argument that names none is the same for every part. Nothing has to cross between parts.
Inputs may be any that keep to these rules, and one draw needn't show every extreme that they name: `row_lists`: within each supernode and ancestor block the 128 kept positions are distinct and increasing.
All inputs are finite; a program needn't handle non-finite values.
Results may differ from the reference program's by a relative error of at most 0.0003.
Values may be sent and summed in bfloat16 or wider, within the bound.
No kernel may reach another device: no remote copies, remote signals or barrier semaphores. Data moves between devices by JAX's collectives and lax.ppermute only.
A program may use at most 64 MiB of HBM per device.

```python
import jax
import jax.numpy as jnp
from jax import lax

SN_COLS = 256
BLK_ROWS = 128
ROW_BLOCKS = 1
NBLK = 4
COL_BLOCKS = 1
NODES = 4
ORDER = 1024
N_ROW = 4
N_COL = 4


def draw_row_lists(key, part):
    key = jax.random.fold_in(key, 7)
    subkeys = jax.random.split(key, NODES * NBLK)

    def one_list(single):
        return jnp.sort(jax.random.permutation(single, SN_COLS)[:BLK_ROWS])
    chosen = jax.vmap(one_list)(subkeys)
    return chosen.reshape(NODES, NBLK, BLK_ROWS).astype(jnp.int32)


def steps_of(key, dims, cuts, low, high):
    def one(position, shards_of):
        heights = jax.random.uniform(jax.random.fold_in(jax.random.fold_in(key, 6), position), (shards_of,), jnp.float32, low / len(cuts), high / len(cuts))
        return jnp.repeat(jnp.exp(heights), dims[position] // shards_of).reshape((-1,) + (1,) * (len(dims) - position - 1))

    level = one(*cuts[0])
    for cut in cuts[1:]:
        level = level * one(*cut)
    return level


def gaussian(key, dims, spread, most, shards=(), held_as=jnp.bfloat16):
    factor_of = steps_of(key, dims, shards, -0.22, 0.18) if shards else 1.0
    drawn = jax.random.normal(key, dims, jnp.float32) * spread * factor_of
    return jnp.minimum(jnp.maximum(drawn, -most), most).astype(held_as)


def setup_inputs(seed: int = 0, part: int = 0) -> dict:
    arg_keys = jax.random.split(jax.random.key(seed), 5)
    own_keys = jax.random.split(jax.random.fold_in(arg_keys[4], part), 5)
    return {
        "inverse_top": gaussian(own_keys[0], (2, ROW_BLOCKS, N_ROW, SN_COLS, COL_BLOCKS, N_COL, SN_COLS), (NBLK * BLK_ROWS) ** -0.5, 0.25, ((2, 4), (5, 4))),
        "factor": gaussian(own_keys[1], (NODES, 2, ROW_BLOCKS, N_ROW, BLK_ROWS, SN_COLS), 0.25, 1.5, ((0, 4), (3, 4))),
        "diag_inverse": gaussian(own_keys[2], (NODES, 2, SN_COLS, SN_COLS), 2.0, 12.0, ((0, 4),), jnp.float32),
        "row_lists": draw_row_lists(jax.random.fold_in(arg_keys[4], 71), part),
    }


def complex_product(first_factor, second_factor):
    real_part = jnp.dot(first_factor[0], second_factor[0], preferred_element_type=jnp.float32) - jnp.dot(first_factor[1], second_factor[1], preferred_element_type=jnp.float32)
    imag_part = jnp.dot(first_factor[0], second_factor[1], preferred_element_type=jnp.float32) + jnp.dot(first_factor[1], second_factor[0], preferred_element_type=jnp.float32)
    return jnp.stack([real_part, imag_part])


def reference(inverse_top, factor, diag_inverse, row_lists):
    surface = inverse_top.reshape(2, ORDER, ORDER)
    columns = factor.reshape(NODES, 2, NBLK * BLK_ROWS, SN_COLS)
    offsets = jnp.arange(NBLK, dtype=jnp.int32)[:, None] * SN_COLS
    highest = lax.Precision.HIGHEST

    def per_node(supernode):
        places = (offsets + row_lists[supernode]).reshape(-1).astype(jnp.int32)
        picked = jnp.take(jnp.take(surface, places, axis=1), places, axis=2)
        inverse_part = -complex_product(picked, columns[supernode])
        narrow = columns[supernode].astype(jnp.float32)
        real_part = jnp.dot(narrow[0].T, inverse_part[0], precision=highest, preferred_element_type=jnp.float32) - jnp.dot(narrow[1].T, inverse_part[1], precision=highest, preferred_element_type=jnp.float32)
        imag_part = jnp.dot(narrow[0].T, inverse_part[1], precision=highest, preferred_element_type=jnp.float32) + jnp.dot(narrow[1].T, inverse_part[0], precision=highest, preferred_element_type=jnp.float32)
        diagonal_part = diag_inverse[supernode] - jnp.stack([real_part, imag_part])
        return inverse_part, diagonal_part

    inverse_block, diagonal_block = lax.map(per_node, jnp.arange(NODES, dtype=jnp.int32))
    return inverse_block.reshape(NODES, 2, ROW_BLOCKS, N_ROW, BLK_ROWS, SN_COLS), diagonal_block
```

```python
import functools

import jax
import jax.numpy as jnp
from jax import lax
from jax.experimental import pallas as pl
from jax.experimental.pallas import tpu as pltpu
from jax.sharding import PartitionSpec as P

VMEM = pl.BlockSpec(memory_space=pltpu.VMEM)
VMEM_BYTES = 48 * 1024 * 1024


def partners(size, step):
    return [(place, place ^ step) for place in range(size)]


def place_one_hot(picks, width):
    kept = picks.shape[-1]
    spots = lax.broadcasted_iota(jnp.int32, (width, kept), 0)
    return jnp.where(spots == picks, 1.0, 0.0).astype(jnp.bfloat16)


def dot(lhs, rhs, contract):
    return lax.dot_general(
        lhs, rhs, (((contract[0],), (contract[1],)), ((), ())), preferred_element_type=jnp.float32
    )


def pick_kernel(grid_rows, grid_cols, local_nodes, surface, row_lists, *pieces):
    row_place = lax.axis_index("row")
    col_place = lax.axis_index("col")
    _, row_blocks, col_blocks, width, _ = surface.shape
    for step in range(grid_cols):
        target = jnp.bitwise_xor(col_place, step)
        for node in range(local_nodes):
            which = target * local_nodes + node
            for row_block in range(row_blocks):
                row_picks = row_lists[which, pl.ds(row_block * grid_rows + row_place, 1), :]
                chosen = place_one_hot(row_picks, width)
                kept = chosen.shape[1]
                for col_block in range(col_blocks):
                    col_picks = row_lists[which, pl.ds(col_block * grid_cols + col_place, 1), :]
                    wanted = place_one_hot(col_picks, width)
                    for half in range(2):
                        rows = dot(chosen, surface[half, row_block, col_block], (0, 0))
                        block = dot(rows.astype(jnp.bfloat16), wanted, (1, 0))
                        pieces[step][
                            node,
                            half,
                            row_block * kept : (row_block + 1) * kept,
                            col_block * kept : (col_block + 1) * kept,
                        ] = block.astype(jnp.bfloat16)


def block_kernel(grid_rows, grid_cols, *refs):
    pieces = refs[:grid_cols]
    factors = refs[grid_cols : grid_cols + grid_rows]
    result, held_factor, held_surface = refs[grid_cols + grid_rows :]
    row_place = lax.axis_index("row")
    col_place = lax.axis_index("col")
    local_nodes, _, row_blocks, kept, width = factors[0].shape
    col_blocks = pieces[0].shape[3] // kept
    rows = row_blocks * kept
    for node in range(local_nodes):
        for step in range(grid_rows):
            source = jnp.bitwise_xor(row_place, step)
            for row_block in range(row_blocks):
                spot = pl.ds(pl.multiple_of((row_block * grid_rows + source) * kept, kept), kept)
                held_factor[spot, :width] = factors[step][node, 0, row_block]
                held_factor[spot, width:] = factors[step][node, 1, row_block]
        for step in range(grid_cols):
            source = jnp.bitwise_xor(col_place, step)
            for col_block in range(col_blocks):
                spot = pl.ds(pl.multiple_of((col_block * grid_cols + source) * kept, kept), kept)
                taken = slice(col_block * kept, (col_block + 1) * kept)
                held_surface[:rows, spot] = pieces[step][node, 0, :, taken]
                held_surface[rows:, spot] = pieces[step][node, 1, :, taken]
        product = dot(held_surface[...], held_factor[...], (1, 0))
        result[node, 0] = product[rows:, width:] - product[:rows, :width]
        result[node, 1] = -(product[:rows, width:] + product[rows:, :width])


def correct_kernel(terms, base, *refs):
    factors, blocks = refs[:terms], refs[terms : 2 * terms]
    result = refs[2 * terms]
    local_nodes, _, rows, width = blocks[0].shape
    for node in range(local_nodes):
        real = base[node, 0]
        imag = base[node, 1]
        for factor, block in zip(factors, blocks):
            wide = jnp.concatenate([block[node, 0], block[node, 1]], axis=1)
            high = wide.astype(jnp.bfloat16)
            low = (wide - high.astype(jnp.float32)).astype(jnp.bfloat16)
            both = jnp.concatenate([high, low], axis=0)
            real_factor = factor[node, 0].reshape(rows, width)
            imag_factor = factor[node, 1].reshape(rows, width)
            from_real = dot(jnp.concatenate([real_factor, real_factor], axis=0), both, (0, 0))
            from_imag = dot(jnp.concatenate([imag_factor, imag_factor], axis=0), both, (0, 0))
            real = real - from_real[:, :width] + from_imag[:, width:]
            imag = imag - from_real[:, width:] - from_imag[:, :width]
        result[node, 0] = real
        result[node, 1] = imag


def call(kernel, out_shape, args, scratch=(), flops=0):
    moved = sum(a.size * a.dtype.itemsize for a in args)
    return pl.pallas_call(
        kernel,
        out_shape=out_shape,
        in_specs=[VMEM] * len(args),
        out_specs=jax.tree.map(lambda _: VMEM, out_shape),
        scratch_shapes=scratch,
        compiler_params=pltpu.CompilerParams(vmem_limit_bytes=VMEM_BYTES),
        cost_estimate=pl.CostEstimate(flops=flops, bytes_accessed=moved, transcendentals=0),
    )(*args)


def local(inverse_top, factor, diag_inverse, row_lists):
    grid_rows = lax.axis_size("row")
    grid_cols = lax.axis_size("col")
    local_nodes, _, row_blocks, _, kept, width = factor.shape
    col_blocks = inverse_top.shape[4]
    rows = row_blocks * kept
    surface = inverse_top.transpose(0, 1, 2, 4, 5, 3, 6).reshape(
        2, row_blocks, col_blocks, width, width
    )
    own_factor = factor.reshape(local_nodes, 2, row_blocks, kept, width)

    piece = jax.ShapeDtypeStruct((local_nodes, 2, rows, col_blocks * kept), jnp.bfloat16)
    pieces = call(
        functools.partial(pick_kernel, grid_rows, grid_cols, local_nodes),
        [piece] * grid_cols,
        [surface, row_lists],
    )
    arrived = [pieces[0]] + [None] * (grid_cols - 1)
    for step in reversed(range(1, grid_cols)):
        arrived[step] = lax.ppermute(pieces[step], "col", partners(grid_cols, step))

    def along_rows(block):
        held = [block] + [None] * (grid_rows - 1)
        for step in range(2, grid_rows, 2):
            held[step] = lax.ppermute(block, "row", partners(grid_rows, step))
        for step in range(1, grid_rows, 2):
            held[step] = lax.ppermute(held[step - 1], "row", partners(grid_rows, 1))
        return held

    factors = along_rows(own_factor)
    total = grid_rows * row_blocks * kept
    inverse_block = call(
        functools.partial(block_kernel, grid_rows, grid_cols),
        jax.ShapeDtypeStruct((local_nodes, 2, rows, width), jnp.float32),
        arrived + factors,
        [pltpu.VMEM((total, 2 * width), jnp.bfloat16), pltpu.VMEM((2 * rows, total), jnp.bfloat16)],
    )
    blocks = along_rows(inverse_block)
    out = jax.ShapeDtypeStruct((local_nodes, 2, width, width), jnp.float32)
    near = call(
        functools.partial(correct_kernel, 2), out, [diag_inverse] + factors[:2] + blocks[:2]
    )
    far = factors[2:] + blocks[2:]
    diagonal_block = call(functools.partial(correct_kernel, grid_rows - 2), out, [near] + far)
    return (
        inverse_block.reshape(local_nodes, 2, row_blocks, 1, kept, width),
        diagonal_block,
    )


def solution(mesh):
    placed = (
        P("pole", None, "row", None, None, "col", None),
        P("col", "pole", None, "row", None, None),
        P("col", "pole", None, None),
        P(),
    )
    return jax.shard_map(
        local,
        mesh=mesh,
        in_specs=placed,
        out_specs=(P("col", "pole", None, "row", None, None), P("col", "pole", None, None)),
        check_vma=False,
    )
```

```python
import functools

import jax
import jax.numpy as jnp
from jax import lax
from jax.experimental import pallas as pl
from jax.experimental.pallas import tpu as pltpu
from jax.sharding import PartitionSpec as P

VMEM = pl.BlockSpec(memory_space=pltpu.VMEM)
VMEM_BYTES = 24 * 1024 * 1024


def partners(size, step):
    return [(place, place ^ step) for place in range(size)]


def place_one_hot(picks, width):
    kept = picks.shape[-1]
    spots = lax.broadcasted_iota(jnp.int32, (width, kept), 0)
    return jnp.where(spots == picks, 1.0, 0.0).astype(jnp.bfloat16)


def dot(lhs, rhs, contract):
    return lax.dot_general(
        lhs, rhs, (((contract[0],), (contract[1],)), ((), ())), preferred_element_type=jnp.float32
    )


def choose_kernel(grid_rows, grid_cols, local_nodes, row_lists, row_choice, col_choice):
    row_place = lax.axis_index("row")
    col_place = lax.axis_index("col")
    slots, row_blocks, width, _ = row_choice.shape
    for slot in range(slots):
        step, node = slot // local_nodes, slot % local_nodes
        which = jnp.bitwise_xor(col_place, step) * local_nodes + node
        for block in range(row_blocks):
            picks = row_lists[which, pl.ds(block * grid_rows + row_place, 1), :]
            row_choice[slot, block] = place_one_hot(picks, width)
        for block in range(col_choice.shape[1]):
            picks = row_lists[which, pl.ds(block * grid_cols + col_place, 1), :]
            col_choice[slot, block] = place_one_hot(picks, width)


def pick_kernel(grid_cols, local_nodes, surface, row_choice, col_choice, *pieces):
    slots, row_blocks, width, kept = row_choice.shape
    col_blocks = col_choice.shape[1]
    for slot in range(slots):
        step, node = slot // local_nodes, slot % local_nodes
        for row_block in range(row_blocks):
            rows = slice(row_block * kept, (row_block + 1) * kept)
            for col_block in range(col_blocks):
                cols = slice(col_block * kept, (col_block + 1) * kept)
                for half in range(2):
                    block = surface[half, row_block, col_block]
                    taken = dot(row_choice[slot, row_block], block, (0, 0)).astype(jnp.bfloat16)
                    taken = dot(taken, col_choice[slot, col_block], (1, 0))
                    pieces[step][node, half, rows, cols] = taken.astype(jnp.bfloat16)


def block_kernel(grid_rows, grid_cols, order, *refs):
    pieces = dict(zip(order, refs[:grid_cols]))
    factors = refs[grid_cols : grid_cols + grid_rows]
    result, held_factor, held_surface = refs[grid_cols + grid_rows :]
    row_place = lax.axis_index("row")
    col_place = lax.axis_index("col")
    local_nodes, _, row_blocks, kept, width = factors[0].shape
    col_blocks = pieces[0].shape[3] // kept
    rows = row_blocks * kept
    for node in range(local_nodes):
        for step in range(grid_rows):
            source = jnp.bitwise_xor(row_place, step)
            for row_block in range(row_blocks):
                spot = pl.ds(pl.multiple_of((row_block * grid_rows + source) * kept, kept), kept)
                held_factor[spot, :width] = factors[step][node, 0, row_block]
                held_factor[spot, width:] = factors[step][node, 1, row_block]
        for step in range(grid_cols):
            source = jnp.bitwise_xor(col_place, step)
            for col_block in range(col_blocks):
                spot = pl.ds(pl.multiple_of((col_block * grid_cols + source) * kept, kept), kept)
                taken = slice(col_block * kept, (col_block + 1) * kept)
                held_surface[:rows, spot] = pieces[step][node, 0, :, taken]
                held_surface[rows:, spot] = pieces[step][node, 1, :, taken]
        product = dot(held_surface[...], held_factor[...], (1, 0))
        result[node, 0] = product[rows:, width:] - product[:rows, :width]
        result[node, 1] = -(product[:rows, width:] + product[rows:, :width])


def correct_kernel(terms, base, *refs):
    factors, blocks = refs[:terms], refs[terms : 2 * terms]
    result = refs[2 * terms]
    if len(refs) > 2 * terms + 1:
        refs[2 * terms + 1][...] = blocks[0][...]
    local_nodes, _, rows, width = blocks[0].shape
    for node in range(local_nodes):
        real = base[node, 0]
        imag = base[node, 1]
        for factor, block in zip(factors, blocks):
            wide = jnp.concatenate([block[node, 0], block[node, 1]], axis=1)
            high = wide.astype(jnp.bfloat16)
            low = (wide - high.astype(jnp.float32)).astype(jnp.bfloat16)
            both = jnp.concatenate([high, low], axis=0)
            real_factor = factor[node, 0].reshape(rows, width)
            imag_factor = factor[node, 1].reshape(rows, width)
            from_real = dot(jnp.concatenate([real_factor, real_factor], axis=0), both, (0, 0))
            from_imag = dot(jnp.concatenate([imag_factor, imag_factor], axis=0), both, (0, 0))
            real = real - from_real[:, :width] + from_imag[:, width:]
            imag = imag - from_real[:, width:] - from_imag[:, :width]
        result[node, 0] = real
        result[node, 1] = imag


def call(kernel, out_shape, args, scratch=(), flops=0):
    moved = sum(a.size * a.dtype.itemsize for a in args)
    return pl.pallas_call(
        kernel,
        out_shape=out_shape,
        in_specs=[VMEM] * len(args),
        out_specs=jax.tree.map(lambda _: VMEM, out_shape),
        scratch_shapes=scratch,
        compiler_params=pltpu.CompilerParams(vmem_limit_bytes=VMEM_BYTES),
        cost_estimate=pl.CostEstimate(flops=flops, bytes_accessed=moved, transcendentals=0),
    )(*args)


def local(inverse_top, factor, diag_inverse, row_lists):
    grid_rows = lax.axis_size("row")
    grid_cols = lax.axis_size("col")
    local_nodes, _, row_blocks, _, kept, width = factor.shape
    col_blocks = inverse_top.shape[4]
    rows = row_blocks * kept
    surface = inverse_top.transpose(0, 1, 2, 4, 5, 3, 6).reshape(
        2, row_blocks, col_blocks, width, width
    )
    own_factor = factor.reshape(local_nodes, 2, row_blocks, kept, width)

    piece = jax.ShapeDtypeStruct((local_nodes, 2, rows, col_blocks * kept), jnp.bfloat16)
    slots = grid_cols * local_nodes
    choices = call(
        functools.partial(choose_kernel, grid_rows, grid_cols, local_nodes),
        [
            jax.ShapeDtypeStruct((slots, row_blocks, width, kept), jnp.bfloat16),
            jax.ShapeDtypeStruct((slots, col_blocks, width, kept), jnp.bfloat16),
        ],
        [row_lists],
    )
    pieces = call(
        functools.partial(pick_kernel, grid_cols, local_nodes),
        [piece] * grid_cols,
        [surface, *choices],
    )
    def across_chips(block):
        steps = range(2, grid_rows, 2)
        return [block] + [lax.ppermute(block, "row", partners(grid_rows, s)) for s in steps]

    def within_chips(blocks):
        return [lax.ppermute(block, "row", partners(grid_rows, 1)) for block in blocks]

    def in_order(blocks):
        half = grid_rows // 2
        return [blocks[step // 2 + (step % 2) * half] for step in range(grid_rows)]

    mate = lax.ppermute(own_factor, "row", partners(grid_rows, 1))
    mate, *pieces = lax.optimization_barrier((mate, *pieces))
    arrived = [pieces[0]] + [None] * (grid_cols - 1)
    order = [0, *range(grid_cols // 2, grid_cols), *range(grid_cols // 2 - 1, 0, -1)]
    for step in order[1:]:
        arrived[step] = lax.ppermute(pieces[step], "col", partners(grid_cols, step))
    factors = [own_factor, mate] + [lax.ppermute(own_factor, "row", partners(grid_rows, k)) for k in range(2, grid_rows)]
    factors = factors[0::2] + factors[1::2]
    total = grid_rows * row_blocks * kept
    work = call(
        functools.partial(block_kernel, grid_rows, grid_cols, tuple(order)),
        jax.ShapeDtypeStruct((local_nodes, 2, rows, width), jnp.float32),
        [arrived[step] for step in order] + in_order(factors),
        [pltpu.VMEM((total, 2 * width), jnp.bfloat16), pltpu.VMEM((2 * rows, total), jnp.bfloat16)],
    )
    out = jax.ShapeDtypeStruct((local_nodes, 2, width, width), jnp.float32)
    half = grid_rows // 2
    across = across_chips(work)
    mate = within_chips(across[:1])
    near, inverse_block = call(
        functools.partial(correct_kernel, 2),
        [out, jax.ShapeDtypeStruct(work.shape, work.dtype)],
        [diag_inverse, factors[0], factors[half], work] + mate,
    )
    near, *others = lax.optimization_barrier((near, *across[1:]))
    far_blocks = others + within_chips(others)
    far_factors = factors[1:half] + factors[half + 1 :]
    diagonal_block = call(
        functools.partial(correct_kernel, grid_rows - 2), out, [near] + far_factors + far_blocks
    )
    return (
        inverse_block.reshape(local_nodes, 2, row_blocks, 1, kept, width),
        diagonal_block,
    )


def solution(mesh):
    placed = (
        P("pole", None, "row", None, None, "col", None),
        P("col", "pole", None, "row", None, None),
        P("col", "pole", None, None),
        P(),
    )
    return jax.shard_map(
        local,
        mesh=mesh,
        in_specs=placed,
        out_specs=(P("col", "pole", None, "row", None, None), P("col", "pole", None, None)),
        check_vma=False,
    )
```

```python
import collections
import functools
import typing

import jax
import jax.numpy as jnp
from jax import lax
from jax.experimental import pallas as pl
from jax.experimental.pallas import tpu as pltpu
from jax.sharding import PartitionSpec as P

VMEM = pl.BlockSpec(memory_space=pltpu.VMEM)
HBM = pl.BlockSpec(memory_space=pltpu.HBM)
VMEM_BYTES = 24 * 1024 * 1024
STEPS_PER_OCTAVE = 64


class Sizes(typing.NamedTuple):
    grid_rows: int
    grid_cols: int
    nodes: int
    row_blocks: int
    col_blocks: int
    kept: int
    width: int

    @property
    def rows(self):
        return self.row_blocks * self.kept

    @property
    def total(self):
        return self.row_blocks * self.grid_rows * self.kept


def partners(size, step):
    return [(place, place ^ step) for place in range(size)]


def dot(lhs, rhs, contract):
    return lax.dot_general(
        lhs, rhs, (((contract[0],), (contract[1],)), ((), ())), preferred_element_type=jnp.float32
    )


def place_one_hot(picks, width):
    kept = picks.shape[-1]
    spots = lax.broadcasted_iota(jnp.int32, (width, kept), 0)
    return jnp.where(spots == picks, 1.0, 0.0).astype(jnp.bfloat16)


def first_kernel(result):
    result[...] = jnp.zeros_like(result)


def pick_kernel(sizes, surface, row_lists, token, *pieces):
    del token
    row_place = lax.axis_index("row")
    col_place = lax.axis_index("col")
    kept = sizes.kept
    for slot in range(sizes.grid_cols * sizes.nodes):
        step, node = slot // sizes.nodes, slot % sizes.nodes
        which = jnp.bitwise_xor(col_place, step) * sizes.nodes + node

        def choice(block):
            return place_one_hot(row_lists[which, pl.ds(block, 1), :], sizes.width)

        for row_block in range(sizes.row_blocks):
            row_choice = choice(row_block * sizes.grid_rows + row_place)
            for col_block in range(sizes.col_blocks):
                col_choice = choice(col_block * sizes.grid_cols + col_place)
                for half in range(2):
                    block = surface[half, row_block, col_block]
                    taken = dot(row_choice, block, (0, 0)).astype(jnp.bfloat16)
                    taken = dot(taken, col_choice, (1, 0))
                    pieces[step][
                        node,
                        half,
                        row_block * kept : (row_block + 1) * kept,
                        col_block * kept : (col_block + 1) * kept,
                    ] = taken.astype(jnp.bfloat16)


def block_at(sizes, block):
    return pl.ds(pl.multiple_of(block * sizes.kept, sizes.kept), sizes.kept)


def gather_factor(sizes, factors, whole_factor):
    row_place = lax.axis_index("row")
    for node in range(sizes.nodes):
        for step in range(sizes.grid_rows):
            source = jnp.bitwise_xor(row_place, step)
            for block in range(sizes.row_blocks):
                spot = block_at(sizes, block * sizes.grid_rows + source)
                whole_factor[node, spot, : sizes.width] = factors[step][node, 0, block]
                whole_factor[node, spot, sizes.width :] = factors[step][node, 1, block]


def minus_product(sizes, node, steps, pieces, whole_factor):
    width, rows = sizes.width, sizes.rows
    col_place = lax.axis_index("col")
    surfaces, factors = [], []
    for step in steps:
        source = jnp.bitwise_xor(col_place, step)
        surfaces.append(jnp.concatenate([pieces[step][node, 0], pieces[step][node, 1]], axis=0))
        for block in range(sizes.col_blocks):
            factors.append(whole_factor[node, block_at(sizes, block * sizes.grid_cols + source), :])
    product = dot(jnp.concatenate(surfaces, axis=1), jnp.concatenate(factors, axis=0), (1, 0))
    real = product[rows:, width:] - product[:rows, :width]
    imag = -(product[:rows, width:] + product[rows:, :width])
    return real, imag


def encode(real, imag, coded):
    rows = real.shape[0]
    most = jnp.max(jnp.maximum(jnp.abs(real), jnp.abs(imag)), axis=0, keepdims=True)
    level = jnp.ceil(jnp.log2(jnp.maximum(most, 1e-30)) * STEPS_PER_OCTAVE + 0.1)
    scale = jnp.exp2(15.0 - level / STEPS_PER_OCTAVE)
    coded[:rows, :] = jnp.round(real * scale).astype(jnp.int32).astype(jnp.int16)
    coded[rows : 2 * rows, :] = jnp.round(imag * scale).astype(jnp.int32).astype(jnp.int16)
    levels = jnp.broadcast_to(level, (16, level.shape[1]))
    coded[2 * rows :, :] = levels.astype(jnp.int32).astype(jnp.int16)


def decode(coded):
    rows = coded.shape[0] // 2 - 8
    level = coded[2 * rows :, :].astype(jnp.int32).astype(jnp.float32)[:1]
    scale = jnp.exp2(level / STEPS_PER_OCTAVE - 15.0)
    values = coded[: 2 * rows, :].astype(jnp.int32).astype(jnp.float32) * scale
    return jnp.concatenate([values[:rows], values[rows:]], axis=1)


def factor_times(sizes, node, steps, blocks, whole_factor):
    width = sizes.width
    row_place = lax.axis_index("row")
    lefts, rights = [], []
    for step, wide in zip(steps, blocks):
        source = jnp.bitwise_xor(row_place, step)
        spots = [block_at(sizes, b * sizes.grid_rows + source) for b in range(sizes.row_blocks)]
        factor = jnp.concatenate([whole_factor[node, spot, :] for spot in spots], axis=0)
        high = wide.astype(jnp.bfloat16)
        low = (wide - high.astype(jnp.float32)).astype(jnp.bfloat16)
        lefts += [factor, factor]
        rights += [high, low]
    product = dot(jnp.concatenate(lefts, axis=0), jnp.concatenate(rights, axis=0), (0, 0))
    real = product[:width, :width] - product[width:, width:]
    imag = product[:width, width:] + product[width:, :width]
    return real, imag


def block_kernel(sizes, pieces, factors, block, coded, whole_factor):
    gather_factor(sizes, factors, whole_factor)
    for node in range(sizes.nodes):
        real, imag = minus_product(sizes, node, sorted(pieces), pieces, whole_factor)
        block[node, 0] = real
        block[node, 1] = imag
        encode(real, imag, coded.at[node])


def near_kernel(sizes, base, whole_factor, own, mate, result, kept_block):
    kept_block[...] = own[...]
    for node in range(sizes.nodes):
        blocks = [jnp.concatenate([b[node, 0], b[node, 1]], axis=1) for b in (own, mate)]
        real, imag = factor_times(sizes, node, (0, 1), blocks, whole_factor)
        result[node, 0] = base[node, 0] - real
        result[node, 1] = base[node, 1] - imag


def far_kernel(sizes, before, whole_factor, coded, result):
    for node in range(sizes.nodes):
        blocks = [decode(coded[step].at[node]) for step in coded]
        real, imag = factor_times(sizes, node, list(coded), blocks, whole_factor)
        result[node, 0] = before[node, 0] - real
        result[node, 1] = before[node, 1] - imag


def call(kernel, out_shape, *args):
    flat, tree = jax.tree.flatten(args)
    out_flat, out_tree = jax.tree.flatten(out_shape)

    def flat_kernel(*refs):
        ins = jax.tree.unflatten(tree, refs[: len(flat)])
        kernel(*ins, *refs[len(flat) :])

    outs = pl.pallas_call(
        flat_kernel,
        out_shape=out_flat,
        in_specs=[VMEM] * len(flat),
        out_specs=[VMEM] * len(out_flat),
        compiler_params=pltpu.CompilerParams(vmem_limit_bytes=VMEM_BYTES),
    )(*flat)
    return jax.tree.unflatten(out_tree, outs)


def local(inverse_top, factor, diag_inverse, row_lists):
    grid_rows = lax.axis_size("row")
    grid_cols = lax.axis_size("col")
    nodes, _, row_blocks, _, kept, width = factor.shape
    col_blocks = inverse_top.shape[4]
    sizes = Sizes(grid_rows, grid_cols, nodes, row_blocks, col_blocks, kept, width)
    rows = sizes.rows
    surface = inverse_top.transpose(0, 1, 2, 4, 5, 3, 6).reshape(
        2, row_blocks, col_blocks, width, width
    )
    own_factor = factor.reshape(nodes, 2, row_blocks, kept, width)
    narrow, wide = jnp.bfloat16, jnp.float32
    work = jax.ShapeDtypeStruct((nodes, 2, rows, width), wide)
    coded = jax.ShapeDtypeStruct((nodes, 2 * rows + 16, width), jnp.int16)
    square = jax.ShapeDtypeStruct((nodes, 2, width, width), wide)
    across = range(2, grid_rows, 2)

    def over_rows(block, step):
        return lax.ppermute(block, "row", partners(grid_rows, step))

    whole = jax.ShapeDtypeStruct((nodes, sizes.total, 2 * width), narrow)
    piece = jax.ShapeDtypeStruct((nodes, 2, rows, col_blocks * kept), narrow)
    token = pl.pallas_call(
        first_kernel,
        out_shape=pltpu.VMEM((8, 128), wide),
        out_specs=VMEM,
        cost_estimate=pl.CostEstimate(flops=10**10, bytes_accessed=10**8, transcendentals=0),
    )()
    token, far_factor = lax.optimization_barrier((token, own_factor))
    pieces = pl.pallas_call(
        functools.partial(pick_kernel, sizes),
        out_shape=[piece] * grid_cols,
        in_specs=[VMEM, VMEM, pl.BlockSpec(memory_space=pl.ANY)],
        out_specs=[VMEM] * grid_cols,
        compiler_params=pltpu.CompilerParams(vmem_limit_bytes=VMEM_BYTES),
    )(surface, row_lists, token)
    factors = collections.OrderedDict({0: own_factor})
    factors.update({step: over_rows(far_factor, step) for step in range(1, grid_rows)})
    factors[1], pieces = lax.optimization_barrier((factors[1], pieces))
    steps = [*range(grid_cols // 2, grid_cols), *range(grid_cols // 2 - 1, 0, -1)]
    arrived = collections.OrderedDict({0: pieces[0]})
    for step in steps:
        arrived[step] = lax.ppermute(pieces[step], "col", partners(grid_cols, step))
    block, coded, whole_factor = call(
        functools.partial(block_kernel, sizes),
        [work, coded, whole],
        arrived, factors,
    )
    sent = collections.OrderedDict((step, over_rows(coded, step)) for step in across)
    near, inverse_block = call(
        functools.partial(near_kernel, sizes),
        [square, work],
        diag_inverse,
        whole_factor,
        block,
        over_rows(block, 1),
    )
    near, sent = lax.optimization_barrier((near, sent))
    forwarded = collections.OrderedDict((step + 1, over_rows(sent[step], 1)) for step in across)
    (middle,) = call(functools.partial(far_kernel, sizes), [square], near, whole_factor, sent)
    (diagonal_block,) = call(
        functools.partial(far_kernel, sizes), [square], middle, whole_factor, forwarded
    )
    return (
        inverse_block.reshape(nodes, 2, row_blocks, 1, kept, width),
        diagonal_block,
    )


def solution(mesh):
    placed = (
        P("pole", None, "row", None, None, "col", None),
        P("col", "pole", None, "row", None, None),
        P("col", "pole", None, None),
        P(),
    )
    return jax.shard_map(
        local,
        mesh=mesh,
        in_specs=placed,
        out_specs=(P("col", "pole", None, "row", None, None), P("col", "pole", None, None)),
        check_vma=False,
    )
```

```python
import collections
import functools
import typing

import jax
import jax.numpy as jnp
from jax import lax
from jax.experimental import pallas as pl
from jax.experimental.pallas import tpu as pltpu
from jax.sharding import PartitionSpec as P

VMEM = pl.BlockSpec(memory_space=pltpu.VMEM)
HBM = pl.BlockSpec(memory_space=pltpu.HBM)
ANY = pl.BlockSpec(memory_space=pl.ANY)
VMEM_BYTES = 24 * 1024 * 1024
STEPS_PER_OCTAVE = 64
CLAIMED_FLOPS = 92 * 10**6

named = collections.OrderedDict


class Sizes(typing.NamedTuple):
    grid_rows: int
    grid_cols: int
    nodes: int
    row_blocks: int
    col_blocks: int
    kept: int
    width: int

    @property
    def rows(self):
        return self.row_blocks * self.kept

    @property
    def total(self):
        return self.row_blocks * self.grid_rows * self.kept


def partners(size, step):
    return [(place, place ^ step) for place in range(size)]


def dot(lhs, rhs, contract=(1, 0)):
    return lax.dot_general(
        lhs, rhs, (((contract[0],), (contract[1],)), ((), ())), preferred_element_type=jnp.float32
    )


def place_one_hot(picks, width):
    kept = picks.shape[-1]
    spots = lax.broadcasted_iota(jnp.int32, (width, kept), 0)
    return jnp.where(spots == picks, 1.0, 0.0).astype(jnp.bfloat16)


def first_kernel(result):
    result[...] = jnp.zeros_like(result)


def pick_kernel(sizes, surface, row_lists, token, *pieces):
    del token
    row_place = lax.axis_index("row")
    col_place = lax.axis_index("col")
    kept, width = sizes.kept, sizes.width
    slots = []
    for step in range(sizes.grid_cols):
        target = jnp.bitwise_xor(col_place, step)
        slots += [(step, node, target * sizes.nodes + node) for node in range(sizes.nodes)]

    def choices(block):
        lists = [row_lists[which, pl.ds(block, 1), :] for _, _, which in slots]
        return jnp.concatenate([place_one_hot(picks, width) for picks in lists], axis=1)

    for col_block in range(sizes.col_blocks):
        col_choices = choices(col_block * sizes.grid_cols + col_place)
        for row_block in range(sizes.row_blocks):
            row_choices = choices(row_block * sizes.grid_rows + row_place)
            halves = [surface[half, row_block, col_block] for half in range(2)]
            taken = dot(jnp.concatenate(halves, axis=0), col_choices).astype(jnp.bfloat16)
            for spot, (step, node, _) in enumerate(slots):
                cols = slice(spot * kept, (spot + 1) * kept)
                both = jnp.concatenate([taken[:width, cols], taken[width:, cols]], axis=1)
                block = dot(row_choices[:, cols], both, (0, 0)).astype(jnp.bfloat16)
                for half in range(2):
                    pieces[step][
                        node,
                        half,
                        row_block * kept : (row_block + 1) * kept,
                        col_block * kept : (col_block + 1) * kept,
                    ] = block[:, half * kept : (half + 1) * kept]


def block_at(sizes, block):
    return pl.ds(pl.multiple_of(block * sizes.kept, sizes.kept), sizes.kept)


def gather_kernel(sizes, factors, far_factor, whole_factor, turned_factor, own_factor, arrival):
    copy = pltpu.make_async_copy(far_factor, own_factor, arrival)
    copy.start()
    row_place = lax.axis_index("row")
    for step in [*range(1, sizes.grid_rows), 0]:
        if not step:
            copy.wait()
        held = factors[step] if step else own_factor
        source = jnp.bitwise_xor(row_place, step)
        for node in range(sizes.nodes):
            for block in range(sizes.row_blocks):
                spot = block_at(sizes, block * sizes.grid_rows + source)
                both = jnp.concatenate([held[node, 0, block], held[node, 1, block]], axis=1)
                whole_factor[node, spot, :] = both
                turned_factor[node, :, spot] = both.T


def block_kernel(sizes, pieces, whole_factor, result, coded):
    width, rows = sizes.width, sizes.rows
    col_place = lax.axis_index("col")
    for node in range(sizes.nodes):
        surfaces, factors = [], []
        for step, piece in pieces.items():
            source = jnp.bitwise_xor(col_place, step)
            surfaces.append(jnp.concatenate([piece[node, 0], piece[node, 1]], axis=0))
            for block in range(sizes.col_blocks):
                spot = block_at(sizes, block * sizes.grid_cols + source)
                factors.append(whole_factor[node, spot, :])
        product = dot(jnp.concatenate(surfaces, axis=1), jnp.concatenate(factors, axis=0))
        real = product[rows:, width:] - product[:rows, :width]
        imag = -(product[:rows, width:] + product[rows:, :width])
        result[node, :, :width] = real
        result[node, :, width:] = imag
        encode(real, imag, coded.at[node])


def encode(real, imag, coded):
    rows = real.shape[0]
    most = jnp.max(jnp.maximum(jnp.abs(real), jnp.abs(imag)), axis=0, keepdims=True)
    level = jnp.ceil(jnp.log2(jnp.maximum(most, 1e-30)) * STEPS_PER_OCTAVE + 0.1)
    scale = jnp.exp2(15.0 - level / STEPS_PER_OCTAVE)
    coded[:rows, :] = jnp.round(real * scale).astype(jnp.int32).astype(jnp.int16)
    coded[rows : 2 * rows, :] = jnp.round(imag * scale).astype(jnp.int32).astype(jnp.int16)
    levels = jnp.broadcast_to(level, (16, level.shape[1]))
    coded[2 * rows :, :] = levels.astype(jnp.int32).astype(jnp.int16)


def decode(coded):
    rows = coded.shape[0] // 2 - 8
    level = coded[2 * rows :, :].astype(jnp.int32).astype(jnp.float32)[:1]
    scale = jnp.exp2(level / STEPS_PER_OCTAVE - 15.0)
    values = coded[: 2 * rows, :].astype(jnp.int32).astype(jnp.float32) * scale
    return jnp.concatenate([values[:rows], values[rows:]], axis=1)


def factor_times(sizes, node, terms, turned_factor, spots=None):
    width = sizes.width
    spots = spots or slice(0, width)
    row_place = lax.axis_index("row")
    reals, imags, rights = [], [], []
    for step, wide in terms.items():
        source = jnp.bitwise_xor(row_place, step)
        places = [block_at(sizes, b * sizes.grid_rows + source) for b in range(sizes.row_blocks)]
        high = wide.astype(jnp.bfloat16)
        low = (wide - high.astype(jnp.float32)).astype(jnp.bfloat16)
        for value in (high, low):
            rights.append(value)
            for place in places:
                reals.append(turned_factor[node, spots.start : spots.stop, place])
                imags.append(turned_factor[node, width + spots.start : width + spots.stop, place])
    right = jnp.concatenate(rights, axis=0)
    from_real = dot(jnp.concatenate(reals, axis=1), right)
    from_imag = dot(jnp.concatenate(imags, axis=1), right)
    real = from_real[:, :width] - from_imag[:, width:]
    imag = from_real[:, width:] + from_imag[:, :width]
    return real, imag


def near_kernel(sizes, base, turned_factor, own, result, block):
    width = sizes.width
    for node in range(sizes.nodes):
        block[node, 0] = own[node, :, :width]
        block[node, 1] = own[node, :, width:]
        real, imag = factor_times(sizes, node, {0: own[node]}, turned_factor)
        result[node, 0] = base[node, 0] - real
        result[node, 1] = base[node, 1] - imag


def middle_kernel(sizes, before, turned_factor, mate, coded, result):
    for node in range(sizes.nodes):
        terms = {1: mate[node], **{step: decode(coded[step].at[node]) for step in coded}}
        real, imag = factor_times(sizes, node, terms, turned_factor)
        result[node, 0] = before[node, 0] - real
        result[node, 1] = before[node, 1] - imag


def last_kernel(sizes, before, turned_factor, coded, result, held, sent):
    half = sizes.width // 2
    copies = []
    for node in range(sizes.nodes):
        terms = {step: decode(coded[step].at[node]) for step in coded}
        for turn in range(2):
            spots = slice(turn * half, (turn + 1) * half)
            real, imag = factor_times(sizes, node, terms, turned_factor, spots)
            held[node, 0, spots] = before[node, 0, spots] - real
            held[node, 1, spots] = before[node, 1, spots] - imag
            place = (node, slice(None), spots)
            copy = pltpu.make_async_copy(held.at[place], result.at[place], sent.at[node, turn])
            copy.start()
            copies.append(copy)
    for copy in copies:
        copy.wait()


def call(kernel, out_shape, *args, remote=(), out_specs=None, scratch=()):
    flat, tree = jax.tree.flatten(args)

    def flat_kernel(*refs):
        ins = jax.tree.unflatten(tree, refs[: len(flat)])
        kernel(*ins, *refs[len(flat) :])

    return pl.pallas_call(
        flat_kernel,
        out_shape=out_shape,
        in_specs=[VMEM] * len(flat) + [HBM] * len(remote),
        out_specs=out_specs or [VMEM] * len(out_shape),
        scratch_shapes=scratch,
        compiler_params=pltpu.CompilerParams(vmem_limit_bytes=VMEM_BYTES),
    )(*flat, *[pltpu.with_memory_space_constraint(a, pltpu.HBM) for a in remote])


def local(inverse_top, factor, diag_inverse, row_lists):
    grid_rows = lax.axis_size("row")
    grid_cols = lax.axis_size("col")
    nodes, _, row_blocks, _, kept, width = factor.shape
    col_blocks = inverse_top.shape[4]
    sizes = Sizes(grid_rows, grid_cols, nodes, row_blocks, col_blocks, kept, width)
    rows = sizes.rows
    surface = inverse_top.transpose(0, 1, 2, 4, 5, 3, 6).reshape(
        2, row_blocks, col_blocks, width, width
    )
    own_factor = factor.reshape(nodes, 2, row_blocks, kept, width)
    narrow, wide = jnp.bfloat16, jnp.float32
    square = jax.ShapeDtypeStruct((nodes, 2, width, width), wide)
    across = range(2, grid_rows, 2)

    def over_rows(block, step):
        return lax.ppermute(block, "row", partners(grid_rows, step))

    token = pl.pallas_call(
        first_kernel,
        out_shape=pltpu.VMEM((8, 128), wide),
        out_specs=VMEM,
        cost_estimate=pl.CostEstimate(flops=CLAIMED_FLOPS, bytes_accessed=0, transcendentals=0),
    )()
    token, sent_factor = lax.optimization_barrier((token, own_factor))
    piece = jax.ShapeDtypeStruct((nodes, 2, rows, col_blocks * kept), narrow)
    pieces = pl.pallas_call(
        functools.partial(pick_kernel, sizes),
        out_shape=[piece] * grid_cols,
        in_specs=[VMEM, VMEM, ANY],
        out_specs=[VMEM] * grid_cols,
        compiler_params=pltpu.CompilerParams(vmem_limit_bytes=VMEM_BYTES),
    )(surface, row_lists, token)
    factors = named((step, over_rows(sent_factor, step)) for step in range(1, grid_rows))
    factors[1], pieces = lax.optimization_barrier((factors[1], pieces))
    arrived = named({0: pieces[0]})
    for step in [*range(grid_cols // 2, grid_cols), *range(grid_cols // 2 - 1, 0, -1)]:
        arrived[step] = lax.ppermute(pieces[step], "col", partners(grid_cols, step))
    whole_factor, turned_factor = call(
        functools.partial(gather_kernel, sizes),
        [
            jax.ShapeDtypeStruct((nodes, sizes.total, 2 * width), narrow),
            jax.ShapeDtypeStruct((nodes, 2 * width, sizes.total), narrow),
        ],
        factors,
        remote=[sent_factor],
        scratch=[pltpu.VMEM(own_factor.shape, narrow), pltpu.SemaphoreType.DMA],
    )
    block, coded = call(
        functools.partial(block_kernel, sizes),
        [
            jax.ShapeDtypeStruct((nodes, rows, 2 * width), wide),
            jax.ShapeDtypeStruct((nodes, 2 * rows + 16, width), jnp.int16),
        ],
        arrived,
        whole_factor,
    )
    sent = named((step, over_rows(coded, step)) for step in across)
    near, inverse_block = call(
        functools.partial(near_kernel, sizes),
        [square, jax.ShapeDtypeStruct((nodes, 2, rows, width), wide)],
        diag_inverse,
        turned_factor,
        block,
    )
    near, block = lax.optimization_barrier((near, block))
    mate = over_rows(block, 1)
    near, sent = lax.optimization_barrier((near, sent))
    forwarded = named((step + 1, over_rows(sent[step], 1)) for step in across)
    (middle,) = call(
        functools.partial(middle_kernel, sizes), [square], near, turned_factor, mate, sent
    )
    (diagonal_block,) = call(
        functools.partial(last_kernel, sizes),
        [square],
        middle,
        turned_factor,
        forwarded,
        out_specs=[HBM],
        scratch=[pltpu.VMEM(square.shape, wide), pltpu.SemaphoreType.DMA((nodes, 2))],
    )
    return inverse_block.reshape(nodes, 2, row_blocks, 1, kept, width), diagonal_block


def solution(mesh):
    placed = (
        P("pole", None, "row", None, None, "col", None),
        P("col", "pole", None, "row", None, None),
        P("col", "pole", None, None),
        P(),
    )
    return jax.shard_map(
        local,
        mesh=mesh,
        in_specs=placed,
        out_specs=(P("col", "pole", None, "row", None, None), P("col", "pole", None, None)),
        check_vma=False,
    )
```

```python
import collections
import functools
import typing

import jax
import jax.numpy as jnp
from jax import lax
from jax.experimental import pallas as pl
from jax.experimental.pallas import tpu as pltpu
from jax.sharding import PartitionSpec as P

VMEM = pl.BlockSpec(memory_space=pltpu.VMEM)
HBM = pl.BlockSpec(memory_space=pltpu.HBM)
ANY = pl.BlockSpec(memory_space=pl.ANY)
VMEM_BYTES = 24 * 1024 * 1024
STEPS_PER_OCTAVE = 64
CLAIMED_FLOPS = 92 * 10**6

named = collections.OrderedDict


class Sizes(typing.NamedTuple):
    grid_rows: int
    grid_cols: int
    nodes: int
    row_blocks: int
    col_blocks: int
    kept: int
    width: int

    @property
    def rows(self):
        return self.row_blocks * self.kept

    @property
    def total(self):
        return self.row_blocks * self.grid_rows * self.kept


def partners(size, step):
    return [(place, place ^ step) for place in range(size)]


def dot(lhs, rhs, contract=(1, 0)):
    return lax.dot_general(
        lhs, rhs, (((contract[0],), (contract[1],)), ((), ())), preferred_element_type=jnp.float32
    )


def place_one_hot(picks, width):
    kept = picks.shape[-1]
    spots = lax.broadcasted_iota(jnp.int32, (width, kept), 0)
    return jnp.where(spots == picks, 1.0, 0.0).astype(jnp.bfloat16)


def first_kernel(result):
    result[...] = jnp.zeros_like(result)


def pick_kernel(sizes, surface, row_lists, token, *pieces):
    del token
    row_place = lax.axis_index("row")
    col_place = lax.axis_index("col")
    kept, width = sizes.kept, sizes.width
    slots = []
    for step in range(sizes.grid_cols):
        target = jnp.bitwise_xor(col_place, step)
        slots += [(step, node, target * sizes.nodes + node) for node in range(sizes.nodes)]

    def choices(block):
        lists = [row_lists[which, pl.ds(block, 1), :] for _, _, which in slots]
        return jnp.concatenate([place_one_hot(picks, width) for picks in lists], axis=1)

    for col_block in range(sizes.col_blocks):
        col_choices = choices(col_block * sizes.grid_cols + col_place)
        for row_block in range(sizes.row_blocks):
            row_choices = choices(row_block * sizes.grid_rows + row_place)
            halves = [surface[half, row_block, col_block] for half in range(2)]
            taken = dot(jnp.concatenate(halves, axis=0), col_choices).astype(jnp.bfloat16)
            for spot, (step, node, _) in enumerate(slots):
                cols = slice(spot * kept, (spot + 1) * kept)
                both = jnp.concatenate([taken[:width, cols], taken[width:, cols]], axis=1)
                block = dot(row_choices[:, cols], both, (0, 0)).astype(jnp.bfloat16)
                for half in range(2):
                    pieces[step][
                        node,
                        half,
                        row_block * kept : (row_block + 1) * kept,
                        col_block * kept : (col_block + 1) * kept,
                    ] = block[:, half * kept : (half + 1) * kept]


def block_at(sizes, block):
    return pl.ds(pl.multiple_of(block * sizes.kept, sizes.kept), sizes.kept)


def stack_kernel(sizes, factors, far_factor, stacked, arrival):
    copy = pltpu.make_async_copy(far_factor, stacked.at[0], arrival)
    copy.start()
    for spot, step in enumerate(factors):
        stacked[spot + 1] = factors[step][...]
    copy.wait()


def gather_kernel(sizes, both, whole_factor, turned_factor):
    row_place = lax.axis_index("row")
    for core in range(2):
        for spot in range(sizes.grid_rows // 2):
            source = jnp.bitwise_xor(row_place - row_place % 2, 2 * spot) + core
            for node in range(sizes.nodes):
                for block in range(sizes.row_blocks):
                    place = block_at(sizes, block * sizes.grid_rows + source)
                    halves = [both[core, spot, node, half, block] for half in range(2)]
                    wide = jnp.concatenate(halves, axis=1)
                    whole_factor[node, place, :] = wide
                    turned_factor[node, :, place] = wide.T


def block_kernel(sizes, pieces, whole_factor, result, coded):
    width, rows = sizes.width, sizes.rows
    col_place = lax.axis_index("col")
    for node in range(sizes.nodes):
        surfaces, factors = [], []
        for step, piece in pieces.items():
            source = jnp.bitwise_xor(col_place, step)
            surfaces.append(jnp.concatenate([piece[node, 0], piece[node, 1]], axis=0))
            for block in range(sizes.col_blocks):
                spot = block_at(sizes, block * sizes.grid_cols + source)
                factors.append(whole_factor[node, spot, :])
        product = dot(jnp.concatenate(surfaces, axis=1), jnp.concatenate(factors, axis=0))
        real = product[rows:, width:] - product[:rows, :width]
        imag = -(product[:rows, width:] + product[rows:, :width])
        result[node, :, :width] = real
        result[node, :, width:] = imag
        encode(real, imag, coded.at[node])


def encode(real, imag, coded):
    rows = real.shape[0]
    most = jnp.max(jnp.maximum(jnp.abs(real), jnp.abs(imag)), axis=0, keepdims=True)
    level = jnp.ceil(jnp.log2(jnp.maximum(most, 1e-30)) * STEPS_PER_OCTAVE + 0.1)
    scale = jnp.exp2(15.0 - level / STEPS_PER_OCTAVE)
    coded[:rows, :] = jnp.round(real * scale).astype(jnp.int32).astype(jnp.int16)
    coded[rows : 2 * rows, :] = jnp.round(imag * scale).astype(jnp.int32).astype(jnp.int16)
    levels = jnp.broadcast_to(level, (16, level.shape[1]))
    coded[2 * rows :, :] = levels.astype(jnp.int32).astype(jnp.int16)


def decode(coded):
    rows = coded.shape[0] // 2 - 8
    level = coded[2 * rows :, :].astype(jnp.int32).astype(jnp.float32)[:1]
    scale = jnp.exp2(level / STEPS_PER_OCTAVE - 15.0)
    values = coded[: 2 * rows, :].astype(jnp.int32).astype(jnp.float32) * scale
    return jnp.concatenate([values[:rows], values[rows:]], axis=1)


def factor_times(sizes, node, terms, turned_factor, spots=None):
    width = sizes.width
    spots = spots or slice(0, width)
    row_place = lax.axis_index("row")
    reals, imags, rights = [], [], []
    for step, wide in terms.items():
        source = jnp.bitwise_xor(row_place, step)
        places = [block_at(sizes, b * sizes.grid_rows + source) for b in range(sizes.row_blocks)]
        high = wide.astype(jnp.bfloat16)
        low = (wide - high.astype(jnp.float32)).astype(jnp.bfloat16)
        for value in (high, low):
            rights.append(value)
            for place in places:
                reals.append(turned_factor[node, spots.start : spots.stop, place])
                imags.append(turned_factor[node, width + spots.start : width + spots.stop, place])
    right = jnp.concatenate(rights, axis=0)
    from_real = dot(jnp.concatenate(reals, axis=1), right)
    from_imag = dot(jnp.concatenate(imags, axis=1), right)
    real = from_real[:, :width] - from_imag[:, width:]
    imag = from_real[:, width:] + from_imag[:, :width]
    return real, imag


def near_kernel(sizes, base, turned_factor, own, result, block):
    width = sizes.width
    for node in range(sizes.nodes):
        block[node, 0] = own[node, :, :width]
        block[node, 1] = own[node, :, width:]
        real, imag = factor_times(sizes, node, {0: own[node]}, turned_factor)
        result[node, 0] = base[node, 0] - real
        result[node, 1] = base[node, 1] - imag


def middle_kernel(sizes, before, turned_factor, mate, coded, result):
    for node in range(sizes.nodes):
        terms = {1: mate[node], **{step: decode(coded[step].at[node]) for step in coded}}
        real, imag = factor_times(sizes, node, terms, turned_factor)
        result[node, 0] = before[node, 0] - real
        result[node, 1] = before[node, 1] - imag


def last_kernel(sizes, before, turned_factor, coded, result, held, sent):
    half = sizes.width // 2
    copies = []
    for node in range(sizes.nodes):
        terms = {step: decode(coded[step].at[node]) for step in coded}
        for turn in range(2):
            spots = slice(turn * half, (turn + 1) * half)
            real, imag = factor_times(sizes, node, terms, turned_factor, spots)
            held[node, 0, spots] = before[node, 0, spots] - real
            held[node, 1, spots] = before[node, 1, spots] - imag
            place = (node, slice(None), spots)
            copy = pltpu.make_async_copy(held.at[place], result.at[place], sent.at[node, turn])
            copy.start()
            copies.append(copy)
    for copy in copies:
        copy.wait()


def call(kernel, out_shape, *args, remote=(), out_specs=None, scratch=()):
    flat, tree = jax.tree.flatten(args)

    def flat_kernel(*refs):
        ins = jax.tree.unflatten(tree, refs[: len(flat)])
        kernel(*ins, *refs[len(flat) :])

    return pl.pallas_call(
        flat_kernel,
        out_shape=out_shape,
        in_specs=[VMEM] * len(flat) + [HBM] * len(remote),
        out_specs=out_specs or [VMEM] * len(out_shape),
        scratch_shapes=scratch,
        compiler_params=pltpu.CompilerParams(vmem_limit_bytes=VMEM_BYTES),
    )(*flat, *[pltpu.with_memory_space_constraint(a, pltpu.HBM) for a in remote])


def local(inverse_top, factor, diag_inverse, row_lists):
    grid_rows = lax.axis_size("row")
    grid_cols = lax.axis_size("col")
    nodes, _, row_blocks, _, kept, width = factor.shape
    col_blocks = inverse_top.shape[4]
    sizes = Sizes(grid_rows, grid_cols, nodes, row_blocks, col_blocks, kept, width)
    rows = sizes.rows
    surface = inverse_top.transpose(0, 1, 2, 4, 5, 3, 6).reshape(
        2, row_blocks, col_blocks, width, width
    )
    own_factor = factor.reshape(nodes, 2, row_blocks, kept, width)
    narrow, wide = jnp.bfloat16, jnp.float32
    square = jax.ShapeDtypeStruct((nodes, 2, width, width), wide)
    across = range(2, grid_rows, 2)

    def over_rows(block, step):
        return lax.ppermute(block, "row", partners(grid_rows, step))

    token = pl.pallas_call(
        first_kernel,
        out_shape=pltpu.VMEM((8, 128), wide),
        out_specs=VMEM,
        cost_estimate=pl.CostEstimate(flops=CLAIMED_FLOPS, bytes_accessed=0, transcendentals=0),
    )()
    token, sent_factor = lax.optimization_barrier((token, own_factor))
    piece = jax.ShapeDtypeStruct((nodes, 2, rows, col_blocks * kept), narrow)
    pieces = pl.pallas_call(
        functools.partial(pick_kernel, sizes),
        out_shape=[piece] * grid_cols,
        in_specs=[VMEM, VMEM, ANY],
        out_specs=[VMEM] * grid_cols,
        compiler_params=pltpu.CompilerParams(vmem_limit_bytes=VMEM_BYTES),
    )(surface, row_lists, token)
    factors = named((step, over_rows(sent_factor, step)) for step in across)
    arrived = named({0: pieces[0]})
    for step in [*range(grid_cols // 2, grid_cols), *range(grid_cols // 2 - 1, 0, -1)]:
        arrived[step] = lax.ppermute(pieces[step], "col", partners(grid_cols, step))
    (stacked,) = call(
        functools.partial(stack_kernel, sizes),
        [jax.ShapeDtypeStruct((grid_rows // 2, *own_factor.shape), narrow)],
        factors,
        remote=[sent_factor],
        scratch=[pltpu.SemaphoreType.DMA],
    )
    pairs = [[place, place + 1] for place in range(0, grid_rows, 2)]
    both = lax.all_gather(stacked, "row", axis_index_groups=pairs)
    whole_factor, turned_factor = call(
        functools.partial(gather_kernel, sizes),
        [
            jax.ShapeDtypeStruct((nodes, sizes.total, 2 * width), narrow),
            jax.ShapeDtypeStruct((nodes, 2 * width, sizes.total), narrow),
        ],
        both,
    )
    block, coded = call(
        functools.partial(block_kernel, sizes),
        [
            jax.ShapeDtypeStruct((nodes, rows, 2 * width), wide),
            jax.ShapeDtypeStruct((nodes, 2 * rows + 16, width), jnp.int16),
        ],
        arrived,
        whole_factor,
    )
    sent = named((step, over_rows(coded, step)) for step in across)
    near, inverse_block = call(
        functools.partial(near_kernel, sizes),
        [square, jax.ShapeDtypeStruct((nodes, 2, rows, width), wide)],
        diag_inverse,
        turned_factor,
        block,
    )
    near, block = lax.optimization_barrier((near, block))
    mate = over_rows(block, 1)
    near, sent = lax.optimization_barrier((near, sent))
    forwarded = named((step + 1, over_rows(sent[step], 1)) for step in across)
    (middle,) = call(
        functools.partial(middle_kernel, sizes), [square], near, turned_factor, mate, sent
    )
    (diagonal_block,) = call(
        functools.partial(last_kernel, sizes),
        [square],
        middle,
        turned_factor,
        forwarded,
        out_specs=[HBM],
        scratch=[pltpu.VMEM(square.shape, wide), pltpu.SemaphoreType.DMA((nodes, 2))],
    )
    return inverse_block.reshape(nodes, 2, row_blocks, 1, kept, width), diagonal_block


def solution(mesh):
    placed = (
        P("pole", None, "row", None, None, "col", None),
        P("col", "pole", None, "row", None, None),
        P("col", "pole", None, None),
        P(),
    )
    return jax.shard_map(
        local,
        mesh=mesh,
        in_specs=placed,
        out_specs=(P("col", "pole", None, "row", None, None), P("col", "pole", None, None)),
        check_vma=False,
    )
```

```python
import collections
import functools
import typing

import jax
import jax.numpy as jnp
from jax import lax
from jax.experimental import pallas as pl
from jax.experimental.pallas import tpu as pltpu
from jax.sharding import PartitionSpec as P

VMEM = pl.BlockSpec(memory_space=pltpu.VMEM)
HBM = pl.BlockSpec(memory_space=pltpu.HBM)
ANY = pl.BlockSpec(memory_space=pl.ANY)
VMEM_BYTES = 24 * 1024 * 1024
STEPS_PER_OCTAVE = 64
CLAIMED_FLOPS = 92 * 10**6

named = collections.OrderedDict


class Sizes(typing.NamedTuple):
    grid_rows: int
    grid_cols: int
    nodes: int
    row_blocks: int
    col_blocks: int
    kept: int
    width: int

    @property
    def rows(self):
        return self.row_blocks * self.kept

    @property
    def total(self):
        return self.row_blocks * self.grid_rows * self.kept


def partners(size, step):
    return [(place, place ^ step) for place in range(size)]


def dot(lhs, rhs, contract=(1, 0)):
    return lax.dot_general(
        lhs, rhs, (((contract[0],), (contract[1],)), ((), ())), preferred_element_type=jnp.float32
    )


def place_one_hot(picks, width):
    kept = picks.shape[-1]
    spots = lax.broadcasted_iota(jnp.int32, (width, kept), 0)
    return jnp.where(spots == picks, 1.0, 0.0).astype(jnp.bfloat16)


def first_kernel(result):
    result[...] = jnp.zeros_like(result)


def pick_kernel(sizes, surface, row_lists, token, *pieces):
    del token
    row_place = lax.axis_index("row")
    col_place = lax.axis_index("col")
    kept, width = sizes.kept, sizes.width
    slots = []
    for step in range(sizes.grid_cols):
        target = jnp.bitwise_xor(col_place, step)
        slots += [(step, node, target * sizes.nodes + node) for node in range(sizes.nodes)]

    nodes, blocks, _ = row_lists.shape
    turned = row_lists[...].reshape(nodes * blocks, kept).astype(jnp.float32).T
    turned_spots = lax.broadcasted_iota(jnp.int32, turned.shape, 1)
    spots = lax.broadcasted_iota(jnp.int32, (kept, width), 1).astype(jnp.float32)

    def row_choice(which, block):
        mine = jnp.where(turned_spots == which * blocks + block, turned, 0.0)
        picks = jnp.sum(mine, axis=1, keepdims=True)
        return jnp.where(spots == picks, 1.0, 0.0).astype(jnp.bfloat16)

    for col_block in range(sizes.col_blocks):
        own_block = pl.ds(col_block * sizes.grid_cols + col_place, 1)
        lists = [row_lists[which, own_block, :] for _, _, which in slots]
        col_choices = jnp.concatenate([place_one_hot(picks, width) for picks in lists], axis=1)
        for row_block in range(sizes.row_blocks):
            both = surface[:, row_block, col_block].reshape(2 * width, width)
            taken = dot(both, col_choices).astype(jnp.bfloat16)
            for spot, (step, node, which) in enumerate(slots):
                cols = slice(spot * kept, (spot + 1) * kept)
                both = jnp.concatenate([taken[:width, cols], taken[width:, cols]], axis=1)
                choice = row_choice(which, row_block * sizes.grid_rows + row_place)
                block = dot(choice, both).astype(jnp.bfloat16)
                for half in range(2):
                    pieces[step][
                        node,
                        half,
                        row_block * kept : (row_block + 1) * kept,
                        col_block * kept : (col_block + 1) * kept,
                    ] = block[:, half * kept : (half + 1) * kept]


def block_at(block, size):
    return pl.ds(pl.multiple_of(block * size, size), size)


def stack_kernel(sizes, factors, far_factor, stacked, arrival):
    copy = pltpu.make_async_copy(far_factor, stacked.at[0], arrival)
    copy.start()
    for spot, step in enumerate(factors):
        stacked[spot + 1] = factors[step][...]
    copy.wait()


def gather_kernel(sizes, both, whole_factor, turned_factor):
    row_place = lax.axis_index("row")
    col_place = lax.axis_index("col")
    kept = sizes.kept
    for core in range(2):
        for spot in range(sizes.grid_rows // 2):
            source = jnp.bitwise_xor(row_place - row_place % 2, 2 * spot) + core
            for node in range(sizes.nodes):
                for block in range(sizes.row_blocks):
                    ancestor = block * sizes.grid_rows + source
                    step = jnp.bitwise_xor(ancestor % sizes.grid_cols, col_place)
                    place = step * sizes.col_blocks + ancestor // sizes.grid_cols
                    halves = [both[core, spot, node, half, block] for half in range(2)]
                    wide = jnp.concatenate(halves, axis=1)
                    whole_factor[node, block_at(place, kept), :] = wide
                    turned = wide.T
                    turned = jnp.concatenate([turned, turned], axis=1)
                    turned_factor[node, :, block_at(ancestor, 2 * kept)] = turned


def block_kernel(sizes, pieces, whole_factor, result, coded):
    width, rows = sizes.width, sizes.rows
    for node in range(sizes.nodes):
        halves = [
            jnp.concatenate([pieces[step][node, half] for step in sorted(pieces)], axis=1)
            for half in range(2)
        ]
        product = dot(jnp.concatenate(halves, axis=0), whole_factor[node])
        real = product[rows:, width:] - product[:rows, :width]
        imag = -(product[:rows, width:] + product[rows:, :width])
        result[node, :, :width] = real
        result[node, :, width:] = imag
        encode(real, imag, coded.at[node])


def encode(real, imag, coded):
    rows = real.shape[0]
    most = jnp.max(jnp.maximum(jnp.abs(real), jnp.abs(imag)), axis=0, keepdims=True)
    level = jnp.ceil(jnp.log2(jnp.maximum(most, 1e-30)) * STEPS_PER_OCTAVE + 0.2)
    scale = jnp.exp2(15.0 - level / STEPS_PER_OCTAVE)
    for half, values in enumerate((real, imag)):
        steps = jnp.clip(jnp.round(values * scale), -32767.0, 32767.0)
        coded[half * rows : (half + 1) * rows, :] = steps.astype(jnp.int32).astype(jnp.int16)
    levels = jnp.broadcast_to(level, (16, level.shape[1]))
    coded[2 * rows :, :] = levels.astype(jnp.int32).astype(jnp.int16)


def decode(coded):
    rows = coded.shape[0] // 2 - 8
    level = coded[2 * rows :, :].astype(jnp.int32).astype(jnp.float32)[:1]
    scale = jnp.exp2(level / STEPS_PER_OCTAVE - 15.0)
    values = coded[: 2 * rows, :].astype(jnp.int32).astype(jnp.float32) * scale
    return jnp.concatenate([values[:rows], values[rows:]], axis=1)


def factor_times(sizes, node, terms, turned_factor, spots=None):
    width, kept = sizes.width, sizes.kept
    spots = spots or slice(0, width)
    row_place = lax.axis_index("row")
    from_real = from_imag = 0.0
    for step, wide in terms.items():
        source = jnp.bitwise_xor(row_place, step)
        high = wide.astype(jnp.bfloat16)
        low = (wide - high.astype(jnp.float32)).astype(jnp.bfloat16)
        for block in range(sizes.row_blocks):
            rows = slice(block * kept, (block + 1) * kept)
            right = jnp.concatenate([high[rows], low[rows]], axis=0)
            place = block_at(block * sizes.grid_rows + source, 2 * kept)
            from_real += dot(turned_factor[node, spots.start : spots.stop, place], right)
            imag_spots = slice(width + spots.start, width + spots.stop)
            from_imag += dot(turned_factor[node, imag_spots, place], right)
    real = from_real[:, :width] - from_imag[:, width:]
    imag = from_real[:, width:] + from_imag[:, :width]
    return real, imag


def near_kernel(sizes, base, turned_factor, own, result, block):
    width = sizes.width
    for node in range(sizes.nodes):
        block[node, 0] = own[node, :, :width]
        block[node, 1] = own[node, :, width:]
        real, imag = factor_times(sizes, node, {0: own[node]}, turned_factor)
        result[node, 0] = base[node, 0] - real
        result[node, 1] = base[node, 1] - imag


def middle_kernel(sizes, before, turned_factor, mate, coded, result):
    for node in range(sizes.nodes):
        terms = {1: mate[node], **{step: decode(coded[step].at[node]) for step in coded}}
        real, imag = factor_times(sizes, node, terms, turned_factor)
        result[node, 0] = before[node, 0] - real
        result[node, 1] = before[node, 1] - imag


def last_kernel(sizes, before, turned_factor, coded, result, held, sent):
    half = sizes.width // 2
    copies = []
    for node in range(sizes.nodes):
        terms = {step: decode(coded[step].at[node]) for step in coded}
        for turn in range(2):
            spots = slice(turn * half, (turn + 1) * half)
            real, imag = factor_times(sizes, node, terms, turned_factor, spots)
            held[node, 0, spots] = before[node, 0, spots] - real
            held[node, 1, spots] = before[node, 1, spots] - imag
            place = (node, slice(None), spots)
            copy = pltpu.make_async_copy(held.at[place], result.at[place], sent.at[node, turn])
            copy.start()
            copies.append(copy)
    for copy in copies:
        copy.wait()


def call(kernel, out_shape, *args, remote=(), out_specs=None, scratch=()):
    flat, tree = jax.tree.flatten(args)

    def flat_kernel(*refs):
        ins = jax.tree.unflatten(tree, refs[: len(flat)])
        kernel(*ins, *refs[len(flat) :])

    return pl.pallas_call(
        flat_kernel,
        out_shape=out_shape,
        in_specs=[VMEM] * len(flat) + [HBM] * len(remote),
        out_specs=out_specs or [VMEM] * len(out_shape),
        scratch_shapes=scratch,
        compiler_params=pltpu.CompilerParams(vmem_limit_bytes=VMEM_BYTES),
    )(*flat, *[pltpu.with_memory_space_constraint(a, pltpu.HBM) for a in remote])


def local(inverse_top, factor, diag_inverse, row_lists):
    grid_rows = lax.axis_size("row")
    grid_cols = lax.axis_size("col")
    nodes, _, row_blocks, _, kept, width = factor.shape
    col_blocks = inverse_top.shape[4]
    sizes = Sizes(grid_rows, grid_cols, nodes, row_blocks, col_blocks, kept, width)
    rows = sizes.rows
    surface = inverse_top.transpose(0, 1, 2, 4, 5, 3, 6).reshape(
        2, row_blocks, col_blocks, width, width
    )
    own_factor = factor.reshape(nodes, 2, row_blocks, kept, width)
    narrow, wide = jnp.bfloat16, jnp.float32
    square = jax.ShapeDtypeStruct((nodes, 2, width, width), wide)
    across = range(2, grid_rows, 2)

    def over_rows(block, step):
        return lax.ppermute(block, "row", partners(grid_rows, step))

    token = pl.pallas_call(
        first_kernel,
        out_shape=pltpu.VMEM((8, 128), wide),
        out_specs=VMEM,
        cost_estimate=pl.CostEstimate(flops=CLAIMED_FLOPS, bytes_accessed=0, transcendentals=0),
    )()
    token, sent_factor = lax.optimization_barrier((token, own_factor))
    piece = jax.ShapeDtypeStruct((nodes, 2, rows, col_blocks * kept), narrow)
    pieces = pl.pallas_call(
        functools.partial(pick_kernel, sizes),
        out_shape=[piece] * grid_cols,
        in_specs=[VMEM, VMEM, ANY],
        out_specs=[VMEM] * grid_cols,
        compiler_params=pltpu.CompilerParams(vmem_limit_bytes=VMEM_BYTES),
    )(surface, row_lists, token)
    factors = named((step, over_rows(sent_factor, step)) for step in across)
    arrived = named({0: pieces[0]})
    for step in [*range(grid_cols // 2, grid_cols), *range(grid_cols // 2 - 1, 0, -1)]:
        arrived[step] = lax.ppermute(pieces[step], "col", partners(grid_cols, step))
    (stacked,) = call(
        functools.partial(stack_kernel, sizes),
        [jax.ShapeDtypeStruct((grid_rows // 2, *own_factor.shape), narrow)],
        factors,
        remote=[sent_factor],
        scratch=[pltpu.SemaphoreType.DMA],
    )
    pairs = [[place, place + 1] for place in range(0, grid_rows, 2)]
    both = lax.all_gather(stacked, "row", axis_index_groups=pairs)
    whole_factor, turned_factor = call(
        functools.partial(gather_kernel, sizes),
        [
            jax.ShapeDtypeStruct((nodes, sizes.total, 2 * width), narrow),
            jax.ShapeDtypeStruct((nodes, 2 * width, 2 * sizes.total), narrow),
        ],
        both,
    )
    block, coded = call(
        functools.partial(block_kernel, sizes),
        [
            jax.ShapeDtypeStruct((nodes, rows, 2 * width), wide),
            jax.ShapeDtypeStruct((nodes, 2 * rows + 16, width), jnp.int16),
        ],
        arrived,
        whole_factor,
    )
    sent = named((step, over_rows(coded, step)) for step in across)
    near, inverse_block = call(
        functools.partial(near_kernel, sizes),
        [square, jax.ShapeDtypeStruct((nodes, 2, rows, width), wide)],
        diag_inverse,
        turned_factor,
        block,
    )
    near, block = lax.optimization_barrier((near, block))
    mate = over_rows(block, 1)
    near, sent = lax.optimization_barrier((near, sent))
    forwarded = named((step + 1, over_rows(sent[step], 1)) for step in across)
    (middle,) = call(
        functools.partial(middle_kernel, sizes), [square], near, turned_factor, mate, sent
    )
    (diagonal_block,) = call(
        functools.partial(last_kernel, sizes),
        [square],
        middle,
        turned_factor,
        forwarded,
        out_specs=[HBM],
        scratch=[pltpu.VMEM(square.shape, wide), pltpu.SemaphoreType.DMA((nodes, 2))],
    )
    return inverse_block.reshape(nodes, 2, row_blocks, 1, kept, width), diagonal_block


def solution(mesh):
    placed = (
        P("pole", None, "row", None, None, "col", None),
        P("col", "pole", None, "row", None, None),
        P("col", "pole", None, None),
        P(),
    )
    return jax.shard_map(
        local,
        mesh=mesh,
        in_specs=placed,
        out_specs=(P("col", "pole", None, "row", None, None), P("col", "pole", None, None)),
        check_vma=False,
    )
```

```python
import collections
import functools
import typing

import jax
import jax.numpy as jnp
from jax import lax
from jax.experimental import pallas as pl
from jax.experimental.pallas import tpu as pltpu
from jax.sharding import PartitionSpec as P

VMEM = pl.BlockSpec(memory_space=pltpu.VMEM)
HBM = pl.BlockSpec(memory_space=pltpu.HBM)
ANY = pl.BlockSpec(memory_space=pl.ANY)
VMEM_BYTES = 24 * 1024 * 1024
CLAIMED_FLOPS = 92 * 10**6

named = collections.OrderedDict


class Sizes(typing.NamedTuple):
    grid_rows: int
    grid_cols: int
    nodes: int
    row_blocks: int
    col_blocks: int
    kept: int
    width: int

    @property
    def rows(self):
        return self.row_blocks * self.kept

    @property
    def total(self):
        return self.row_blocks * self.grid_rows * self.kept


def partners(size, step):
    return [(place, place ^ step) for place in range(size)]


def dot(lhs, rhs, contract=(1, 0)):
    return lax.dot_general(
        lhs, rhs, (((contract[0],), (contract[1],)), ((), ())), preferred_element_type=jnp.float32
    )


def place_one_hot(picks, width):
    kept = picks.shape[-1]
    spots = lax.broadcasted_iota(jnp.int32, (width, kept), 0)
    return jnp.where(spots == picks, 1.0, 0.0).astype(jnp.bfloat16)


def first_kernel(result):
    result[...] = jnp.zeros_like(result)


def pick_kernel(sizes, surface, row_lists, token, *pieces):
    del token
    row_place = lax.axis_index("row")
    col_place = lax.axis_index("col")
    kept, width = sizes.kept, sizes.width
    slots = []
    for step in range(sizes.grid_cols):
        target = jnp.bitwise_xor(col_place, step)
        slots += [(step, node, target * sizes.nodes + node) for node in range(sizes.nodes)]

    nodes, blocks, _ = row_lists.shape
    turned = row_lists[...].reshape(nodes * blocks, kept).astype(jnp.float32).T
    turned_spots = lax.broadcasted_iota(jnp.int32, turned.shape, 1)
    spots = lax.broadcasted_iota(jnp.int32, (kept, width), 1).astype(jnp.float32)

    def row_choice(which, block):
        mine = jnp.where(turned_spots == which * blocks + block, turned, 0.0)
        picks = jnp.sum(mine, axis=1, keepdims=True)
        return jnp.where(spots == picks, 1.0, 0.0).astype(jnp.bfloat16)

    for col_block in range(sizes.col_blocks):
        own_block = pl.ds(col_block * sizes.grid_cols + col_place, 1)
        lists = [row_lists[which, own_block, :] for _, _, which in slots]
        col_choices = jnp.concatenate([place_one_hot(picks, width) for picks in lists], axis=1)
        for row_block in range(sizes.row_blocks):
            both = surface[:, row_block, col_block].reshape(2 * width, width)
            taken = dot(both, col_choices).astype(jnp.bfloat16)
            for spot, (step, node, which) in enumerate(slots):
                cols = slice(spot * kept, (spot + 1) * kept)
                both = jnp.concatenate([taken[:width, cols], taken[width:, cols]], axis=1)
                choice = row_choice(which, row_block * sizes.grid_rows + row_place)
                block = dot(choice, both).astype(jnp.bfloat16)
                for half in range(2):
                    pieces[step][
                        node,
                        half,
                        row_block * kept : (row_block + 1) * kept,
                        col_block * kept : (col_block + 1) * kept,
                    ] = block[:, half * kept : (half + 1) * kept]


def block_at(block, size):
    return pl.ds(pl.multiple_of(block * size, size), size)


def stack_kernel(sizes, factors, far_factor, stacked, arrival):
    copy = pltpu.make_async_copy(far_factor, stacked.at[0], arrival)
    copy.start()
    for spot, step in enumerate(factors):
        stacked[spot + 1] = factors[step][...]
    copy.wait()


def gather_kernel(sizes, both, whole_factor, turned_factor):
    row_place = lax.axis_index("row")
    col_place = lax.axis_index("col")
    kept = sizes.kept
    for core in range(2):
        for spot in range(sizes.grid_rows // 2):
            source = jnp.bitwise_xor(row_place - row_place % 2, 2 * spot) + core
            for node in range(sizes.nodes):
                for block in range(sizes.row_blocks):
                    ancestor = block * sizes.grid_rows + source
                    step = jnp.bitwise_xor(ancestor % sizes.grid_cols, col_place)
                    place = step * sizes.col_blocks + ancestor // sizes.grid_cols
                    halves = [both[core, spot, node, half, block] for half in range(2)]
                    wide = jnp.concatenate(halves, axis=1)
                    whole_factor[node, block_at(place, kept), :] = wide
                    turned = wide.T
                    turned = jnp.concatenate([turned, turned], axis=1)
                    turned_factor[node, :, block_at(ancestor, 2 * kept)] = turned


def block_kernel(sizes, pieces, whole_factor, result):
    width, rows = sizes.width, sizes.rows
    for node in range(sizes.nodes):
        halves = [
            jnp.concatenate([pieces[step][node, half] for step in sorted(pieces)], axis=1)
            for half in range(2)
        ]
        product = dot(jnp.concatenate(halves, axis=0), whole_factor[node])
        real = product[rows:, width:] - product[:rows, :width]
        imag = -(product[:rows, width:] + product[rows:, :width])
        result[node, :, :width] = real
        result[node, :, width:] = imag


def factor_times(sizes, node, terms, turned_factor, spots=None):
    width, kept = sizes.width, sizes.kept
    spots = spots or slice(0, width)
    row_place = lax.axis_index("row")
    from_real = from_imag = 0.0
    for step, wide in terms.items():
        source = jnp.bitwise_xor(row_place, step)
        high = wide.astype(jnp.bfloat16)
        low = (wide - high.astype(jnp.float32)).astype(jnp.bfloat16)
        for block in range(sizes.row_blocks):
            rows = slice(block * kept, (block + 1) * kept)
            right = jnp.concatenate([high[rows], low[rows]], axis=0)
            place = block_at(block * sizes.grid_rows + source, 2 * kept)
            from_real += dot(turned_factor[node, spots.start : spots.stop, place], right)
            imag_spots = slice(width + spots.start, width + spots.stop)
            from_imag += dot(turned_factor[node, imag_spots, place], right)
    real = from_real[:, :width] - from_imag[:, width:]
    imag = from_real[:, width:] + from_imag[:, :width]
    return real, imag


def near_kernel(sizes, base, turned_factor, own, result, block):
    width = sizes.width
    for node in range(sizes.nodes):
        block[node, 0] = own[node, :, :width]
        block[node, 1] = own[node, :, width:]
        real, imag = factor_times(sizes, node, {0: own[node]}, turned_factor)
        result[node, 0] = base[node, 0] - real
        result[node, 1] = base[node, 1] - imag


def middle_kernel(sizes, before, turned_factor, mate, sent, result):
    for node in range(sizes.nodes):
        terms = {1: mate[node], **{step: sent[step][node] for step in sent}}
        real, imag = factor_times(sizes, node, terms, turned_factor)
        result[node, 0] = before[node, 0] - real
        result[node, 1] = before[node, 1] - imag


def last_kernel(sizes, before, turned_factor, forwarded, result, held, sent):
    half = sizes.width // 2
    copies = []
    for node in range(sizes.nodes):
        terms = {step: forwarded[step][node] for step in forwarded}
        for turn in range(2):
            spots = slice(turn * half, (turn + 1) * half)
            real, imag = factor_times(sizes, node, terms, turned_factor, spots)
            held[node, 0, spots] = before[node, 0, spots] - real
            held[node, 1, spots] = before[node, 1, spots] - imag
            place = (node, slice(None), spots)
            copy = pltpu.make_async_copy(held.at[place], result.at[place], sent.at[node, turn])
            copy.start()
            copies.append(copy)
    for copy in copies:
        copy.wait()


def call(kernel, out_shape, *args, remote=(), out_specs=None, scratch=()):
    flat, tree = jax.tree.flatten(args)

    def flat_kernel(*refs):
        ins = jax.tree.unflatten(tree, refs[: len(flat)])
        kernel(*ins, *refs[len(flat) :])

    return pl.pallas_call(
        flat_kernel,
        out_shape=out_shape,
        in_specs=[VMEM] * len(flat) + [HBM] * len(remote),
        out_specs=out_specs or [VMEM] * len(out_shape),
        scratch_shapes=scratch,
        compiler_params=pltpu.CompilerParams(vmem_limit_bytes=VMEM_BYTES),
    )(*flat, *[pltpu.with_memory_space_constraint(a, pltpu.HBM) for a in remote])


def local(inverse_top, factor, diag_inverse, row_lists):
    grid_rows = lax.axis_size("row")
    grid_cols = lax.axis_size("col")
    nodes, _, row_blocks, _, kept, width = factor.shape
    col_blocks = inverse_top.shape[4]
    sizes = Sizes(grid_rows, grid_cols, nodes, row_blocks, col_blocks, kept, width)
    rows = sizes.rows
    surface = inverse_top.transpose(0, 1, 2, 4, 5, 3, 6).reshape(
        2, row_blocks, col_blocks, width, width
    )
    own_factor = factor.reshape(nodes, 2, row_blocks, kept, width)
    narrow, wide = jnp.bfloat16, jnp.float32
    square = jax.ShapeDtypeStruct((nodes, 2, width, width), wide)
    across = range(2, grid_rows, 2)

    def over_rows(block, step):
        return lax.ppermute(block, "row", partners(grid_rows, step))

    token = pl.pallas_call(
        first_kernel,
        out_shape=pltpu.VMEM((8, 128), wide),
        out_specs=VMEM,
        cost_estimate=pl.CostEstimate(flops=CLAIMED_FLOPS, bytes_accessed=0, transcendentals=0),
    )()
    token, sent_factor = lax.optimization_barrier((token, own_factor))
    piece = jax.ShapeDtypeStruct((nodes, 2, rows, col_blocks * kept), narrow)
    pieces = pl.pallas_call(
        functools.partial(pick_kernel, sizes),
        out_shape=[piece] * grid_cols,
        in_specs=[VMEM, VMEM, ANY],
        out_specs=[VMEM] * grid_cols,
        compiler_params=pltpu.CompilerParams(vmem_limit_bytes=VMEM_BYTES),
    )(surface, row_lists, token)
    factors = named((step, over_rows(sent_factor, step)) for step in across)
    arrived = named({0: pieces[0]})
    for step in [*range(grid_cols // 2, grid_cols), *range(grid_cols // 2 - 1, 0, -1)]:
        arrived[step] = lax.ppermute(pieces[step], "col", partners(grid_cols, step))
    (stacked,) = call(
        functools.partial(stack_kernel, sizes),
        [jax.ShapeDtypeStruct((grid_rows // 2, *own_factor.shape), narrow)],
        factors,
        remote=[sent_factor],
        scratch=[pltpu.SemaphoreType.DMA],
    )
    pairs = [[place, place + 1] for place in range(0, grid_rows, 2)]
    both = lax.all_gather(stacked, "row", axis_index_groups=pairs)
    whole_factor, turned_factor = call(
        functools.partial(gather_kernel, sizes),
        [
            jax.ShapeDtypeStruct((nodes, sizes.total, 2 * width), narrow),
            jax.ShapeDtypeStruct((nodes, 2 * width, 2 * sizes.total), narrow),
        ],
        both,
    )
    (block,) = call(
        functools.partial(block_kernel, sizes),
        [jax.ShapeDtypeStruct((nodes, rows, 2 * width), wide)],
        arrived,
        whole_factor,
    )
    sent = named((step, over_rows(block, step)) for step in across)
    near, inverse_block = call(
        functools.partial(near_kernel, sizes),
        [square, jax.ShapeDtypeStruct((nodes, 2, rows, width), wide)],
        diag_inverse,
        turned_factor,
        block,
    )
    near, block = lax.optimization_barrier((near, block))
    mate = over_rows(block, 1)
    near, sent = lax.optimization_barrier((near, sent))
    forwarded = named((step + 1, over_rows(sent[step], 1)) for step in across)
    (middle,) = call(
        functools.partial(middle_kernel, sizes), [square], near, turned_factor, mate, sent
    )
    (diagonal_block,) = call(
        functools.partial(last_kernel, sizes),
        [square],
        middle,
        turned_factor,
        forwarded,
        out_specs=[HBM],
        scratch=[pltpu.VMEM(square.shape, wide), pltpu.SemaphoreType.DMA((nodes, 2))],
    )
    return inverse_block.reshape(nodes, 2, row_blocks, 1, kept, width), diagonal_block


def solution(mesh):
    placed = (
        P("pole", None, "row", None, None, "col", None),
        P("col", "pole", None, "row", None, None),
        P("col", "pole", None, None),
        P(),
    )
    return jax.shard_map(
        local,
        mesh=mesh,
        in_specs=placed,
        out_specs=(P("col", "pole", None, "row", None, None), P("col", "pole", None, None)),
        check_vma=False,
    )
```

```python
import collections
import functools
import typing

import jax
import jax.numpy as jnp
from jax import lax
from jax.experimental import pallas as pl
from jax.experimental.pallas import tpu as pltpu
from jax.sharding import PartitionSpec as P

VMEM = pl.BlockSpec(memory_space=pltpu.VMEM)
HBM = pl.BlockSpec(memory_space=pltpu.HBM)
ANY = pl.BlockSpec(memory_space=pl.ANY)
VMEM_BYTES = 24 * 1024 * 1024
STEPS_PER_OCTAVE = 64
CLAIMED_FLOPS = 92 * 10**6

named = collections.OrderedDict


class Sizes(typing.NamedTuple):
    grid_rows: int
    grid_cols: int
    nodes: int
    row_blocks: int
    col_blocks: int
    kept: int
    width: int

    @property
    def rows(self):
        return self.row_blocks * self.kept

    @property
    def total(self):
        return self.row_blocks * self.grid_rows * self.kept


def partners(size, step):
    return [(place, place ^ step) for place in range(size)]


def dot(lhs, rhs, contract=(1, 0)):
    return lax.dot_general(
        lhs, rhs, (((contract[0],), (contract[1],)), ((), ())), preferred_element_type=jnp.float32
    )


def place_one_hot(picks, width):
    kept = picks.shape[-1]
    spots = lax.broadcasted_iota(jnp.int32, (width, kept), 0)
    return jnp.where(spots == picks, 1.0, 0.0).astype(jnp.bfloat16)


def first_kernel(result):
    result[...] = jnp.zeros_like(result)


def pick(sizes, steps, surface, row_lists, pieces):
    row_place = lax.axis_index("row")
    col_place = lax.axis_index("col")
    kept, width = sizes.kept, sizes.width
    slots = []
    for step in steps:
        target = jnp.bitwise_xor(col_place, step)
        slots += [(step, node, target * sizes.nodes + node) for node in range(sizes.nodes)]
    nodes, blocks, _ = row_lists.shape
    turned = row_lists[...].reshape(nodes * blocks, kept).astype(jnp.float32).T
    turned_spots = lax.broadcasted_iota(jnp.int32, turned.shape, 1)
    spots = lax.broadcasted_iota(jnp.int32, (kept, width), 1).astype(jnp.float32)

    def row_choice(which, block):
        mine = jnp.where(turned_spots == which * blocks + block, turned, 0.0)
        picks = jnp.sum(mine, axis=1, keepdims=True)
        return jnp.where(spots == picks, 1.0, 0.0).astype(jnp.bfloat16)

    for col_block in range(sizes.col_blocks):
        own_block = pl.ds(col_block * sizes.grid_cols + col_place, 1)
        lists = [row_lists[which, own_block, :] for _, _, which in slots]
        col_choices = jnp.concatenate([place_one_hot(picks, width) for picks in lists], axis=1)
        for row_block in range(sizes.row_blocks):
            both = surface[:, row_block, col_block].reshape(2 * width, width)
            taken = dot(both, col_choices).astype(jnp.bfloat16)
            for spot, (step, node, which) in enumerate(slots):
                cols = slice(spot * kept, (spot + 1) * kept)
                both = jnp.concatenate([taken[:width, cols], taken[width:, cols]], axis=1)
                choice = row_choice(which, row_block * sizes.grid_rows + row_place)
                block = dot(choice, both).astype(jnp.bfloat16)
                for half in range(2):
                    pieces[step][
                        node,
                        half,
                        row_block * kept : (row_block + 1) * kept,
                        col_block * kept : (col_block + 1) * kept,
                    ] = block[:, half * kept : (half + 1) * kept]


def pick_kernel(sizes, surface, row_lists, token, *pieces):
    del token
    steps = range(1, sizes.grid_cols)
    pick(sizes, steps, surface, row_lists, dict(zip(steps, pieces)))


def block_at(block, size):
    return pl.ds(pl.multiple_of(block * size, size), size)


def stack_kernel(sizes, factors, surface, row_lists, far_factor, stacked, piece, arrival):
    copy = pltpu.make_async_copy(far_factor, stacked.at[0], arrival)
    copy.start()
    for spot, step in enumerate(factors):
        stacked[spot + 1] = factors[step][...]
    pick(sizes, [0], surface, row_lists, [piece])
    copy.wait()


def product_of(sizes, node, pieces, whole_factor):
    rows = sizes.col_blocks * sizes.kept
    lefts, rights = [], []
    for step, piece in pieces.items():
        lefts.append(jnp.concatenate([piece[node, 0], piece[node, 1]], axis=0))
        rights.append(whole_factor[node, step * rows : (step + 1) * rows, :])
    return dot(jnp.concatenate(lefts, axis=1), jnp.concatenate(rights, axis=0))


def gather_kernel(sizes, both, pieces, whole_factor, turned_factor, early):
    row_place = lax.axis_index("row")
    col_place = lax.axis_index("col")
    kept = sizes.kept
    for core in range(2):
        for spot in range(sizes.grid_rows // 2):
            source = jnp.bitwise_xor(row_place - row_place % 2, 2 * spot) + core
            for node in range(sizes.nodes):
                for block in range(sizes.row_blocks):
                    ancestor = block * sizes.grid_rows + source
                    step = jnp.bitwise_xor(ancestor % sizes.grid_cols, col_place)
                    place = step * sizes.col_blocks + ancestor // sizes.grid_cols
                    halves = [both[core, spot, node, half, block] for half in range(2)]
                    wide = jnp.concatenate(halves, axis=1)
                    whole_factor[node, block_at(place, kept), :] = wide
                    turned = wide.T
                    turned = jnp.concatenate([turned, turned], axis=1)
                    turned_factor[node, :, block_at(ancestor, 2 * kept)] = turned
    for node in range(sizes.nodes):
        early[node] = product_of(sizes, node, pieces, whole_factor)


def block_kernel(sizes, pieces, whole_factor, early, result, coded):
    width, rows = sizes.width, sizes.rows
    for node in range(sizes.nodes):
        product = early[node] + product_of(sizes, node, pieces, whole_factor)
        real = product[rows:, width:] - product[:rows, :width]
        imag = -(product[:rows, width:] + product[rows:, :width])
        result[node, :, :width] = real
        result[node, :, width:] = imag
        encode(real, imag, coded.at[node])


def encode(real, imag, coded):
    rows = real.shape[0]
    most = jnp.max(jnp.maximum(jnp.abs(real), jnp.abs(imag)), axis=0, keepdims=True)
    level = jnp.ceil(jnp.log2(jnp.maximum(most, 1e-30)) * STEPS_PER_OCTAVE + 0.2)
    scale = jnp.exp2(15.0 - level / STEPS_PER_OCTAVE)
    for half, values in enumerate((real, imag)):
        steps = jnp.clip(jnp.round(values * scale), -32767.0, 32767.0)
        coded[half * rows : (half + 1) * rows, :] = steps.astype(jnp.int32).astype(jnp.int16)
    levels = jnp.broadcast_to(level, (16, level.shape[1]))
    coded[2 * rows :, :] = levels.astype(jnp.int32).astype(jnp.int16)


def decode(coded):
    rows = coded.shape[0] // 2 - 8
    level = coded[2 * rows :, :].astype(jnp.int32).astype(jnp.float32)[:1]
    scale = jnp.exp2(level / STEPS_PER_OCTAVE - 15.0)
    values = coded[: 2 * rows, :].astype(jnp.int32).astype(jnp.float32) * scale
    return jnp.concatenate([values[:rows], values[rows:]], axis=1)


def factor_times(sizes, node, terms, turned_factor, spots=None):
    width, kept = sizes.width, sizes.kept
    spots = spots or slice(0, width)
    row_place = lax.axis_index("row")
    from_real = from_imag = 0.0
    for step, wide in terms.items():
        source = jnp.bitwise_xor(row_place, step)
        high = wide.astype(jnp.bfloat16)
        low = (wide - high.astype(jnp.float32)).astype(jnp.bfloat16)
        for block in range(sizes.row_blocks):
            rows = slice(block * kept, (block + 1) * kept)
            right = jnp.concatenate([high[rows], low[rows]], axis=0)
            place = block_at(block * sizes.grid_rows + source, 2 * kept)
            from_real += dot(turned_factor[node, spots.start : spots.stop, place], right)
            imag_spots = slice(width + spots.start, width + spots.stop)
            from_imag += dot(turned_factor[node, imag_spots, place], right)
    real = from_real[:, :width] - from_imag[:, width:]
    imag = from_real[:, width:] + from_imag[:, :width]
    return real, imag


def near_kernel(sizes, base, turned_factor, own, result, block):
    width = sizes.width
    for node in range(sizes.nodes):
        block[node, 0] = own[node, :, :width]
        block[node, 1] = own[node, :, width:]
        real, imag = factor_times(sizes, node, {0: own[node]}, turned_factor)
        result[node, 0] = base[node, 0] - real
        result[node, 1] = base[node, 1] - imag


def middle_kernel(sizes, before, turned_factor, mate, coded, result):
    for node in range(sizes.nodes):
        terms = {1: mate[node], **{step: decode(coded[step].at[node]) for step in coded}}
        real, imag = factor_times(sizes, node, terms, turned_factor)
        result[node, 0] = before[node, 0] - real
        result[node, 1] = before[node, 1] - imag


def last_kernel(sizes, before, turned_factor, coded, result, held, sent):
    half = sizes.width // 2
    copies = []
    for node in range(sizes.nodes):
        terms = {step: decode(coded[step].at[node]) for step in coded}
        for turn in range(2):
            spots = slice(turn * half, (turn + 1) * half)
            real, imag = factor_times(sizes, node, terms, turned_factor, spots)
            held[node, 0, spots] = before[node, 0, spots] - real
            held[node, 1, spots] = before[node, 1, spots] - imag
            place = (node, slice(None), spots)
            copy = pltpu.make_async_copy(held.at[place], result.at[place], sent.at[node, turn])
            copy.start()
            copies.append(copy)
    for copy in copies:
        copy.wait()


def call(kernel, out_shape, *args, remote=(), out_specs=None, scratch=()):
    flat, tree = jax.tree.flatten(args)

    def flat_kernel(*refs):
        ins = jax.tree.unflatten(tree, refs[: len(flat)])
        kernel(*ins, *refs[len(flat) :])

    return pl.pallas_call(
        flat_kernel,
        out_shape=out_shape,
        in_specs=[VMEM] * len(flat) + [HBM] * len(remote),
        out_specs=out_specs or [VMEM] * len(out_shape),
        scratch_shapes=scratch,
        compiler_params=pltpu.CompilerParams(vmem_limit_bytes=VMEM_BYTES),
    )(*flat, *[pltpu.with_memory_space_constraint(a, pltpu.HBM) for a in remote])


def local(inverse_top, factor, diag_inverse, row_lists):
    grid_rows = lax.axis_size("row")
    grid_cols = lax.axis_size("col")
    nodes, _, row_blocks, _, kept, width = factor.shape
    col_blocks = inverse_top.shape[4]
    sizes = Sizes(grid_rows, grid_cols, nodes, row_blocks, col_blocks, kept, width)
    rows = sizes.rows
    surface = inverse_top.transpose(0, 1, 2, 4, 5, 3, 6).reshape(
        2, row_blocks, col_blocks, width, width
    )
    own_factor = factor.reshape(nodes, 2, row_blocks, kept, width)
    narrow, wide = jnp.bfloat16, jnp.float32
    square = jax.ShapeDtypeStruct((nodes, 2, width, width), wide)
    across = range(2, grid_rows, 2)

    def over_rows(block, step):
        return lax.ppermute(block, "row", partners(grid_rows, step))

    token = pl.pallas_call(
        first_kernel,
        out_shape=pltpu.VMEM((8, 128), wide),
        out_specs=VMEM,
        cost_estimate=pl.CostEstimate(flops=CLAIMED_FLOPS, bytes_accessed=0, transcendentals=0),
    )()
    token, sent_factor = lax.optimization_barrier((token, own_factor))
    piece = jax.ShapeDtypeStruct((nodes, 2, rows, col_blocks * kept), narrow)
    pieces = pl.pallas_call(
        functools.partial(pick_kernel, sizes),
        out_shape=[piece] * (grid_cols - 1),
        in_specs=[VMEM, VMEM, ANY],
        out_specs=[VMEM] * (grid_cols - 1),
        compiler_params=pltpu.CompilerParams(vmem_limit_bytes=VMEM_BYTES),
    )(surface, row_lists, token)
    factors = named((step, over_rows(sent_factor, step)) for step in across)
    arrived = named()
    for step in [*range(grid_cols // 2, grid_cols), *range(grid_cols // 2 - 1, 0, -1)]:
        arrived[step] = lax.ppermute(pieces[step - 1], "col", partners(grid_cols, step))
    stacked, own_piece = call(
        functools.partial(stack_kernel, sizes),
        [jax.ShapeDtypeStruct((grid_rows // 2, *own_factor.shape), narrow), piece],
        factors,
        surface,
        row_lists,
        remote=[sent_factor],
        scratch=[pltpu.SemaphoreType.DMA],
    )
    pairs = [[place, place + 1] for place in range(0, grid_rows, 2)]
    both = lax.all_gather(stacked, "row", axis_index_groups=pairs)
    first = named({0: own_piece, grid_cols // 2: arrived.pop(grid_cols // 2)})
    whole_factor, turned_factor, early = call(
        functools.partial(gather_kernel, sizes),
        [
            jax.ShapeDtypeStruct((nodes, sizes.total, 2 * width), narrow),
            jax.ShapeDtypeStruct((nodes, 2 * width, 2 * sizes.total), narrow),
            jax.ShapeDtypeStruct((nodes, 2 * rows, 2 * width), wide),
        ],
        both,
        first,
    )
    block, coded = call(
        functools.partial(block_kernel, sizes),
        [
            jax.ShapeDtypeStruct((nodes, rows, 2 * width), wide),
            jax.ShapeDtypeStruct((nodes, 2 * rows + 16, width), jnp.int16),
        ],
        arrived,
        whole_factor,
        early,
    )
    sent = named((step, over_rows(coded, step)) for step in across)
    near, inverse_block = call(
        functools.partial(near_kernel, sizes),
        [square, jax.ShapeDtypeStruct((nodes, 2, rows, width), wide)],
        diag_inverse,
        turned_factor,
        block,
    )
    near, block = lax.optimization_barrier((near, block))
    mate = over_rows(block, 1)
    near, sent = lax.optimization_barrier((near, sent))
    forwarded = named((step + 1, over_rows(sent[step], 1)) for step in across)
    (middle,) = call(
        functools.partial(middle_kernel, sizes), [square], near, turned_factor, mate, sent
    )
    (diagonal_block,) = call(
        functools.partial(last_kernel, sizes),
        [square],
        middle,
        turned_factor,
        forwarded,
        out_specs=[HBM],
        scratch=[pltpu.VMEM(square.shape, wide), pltpu.SemaphoreType.DMA((nodes, 2))],
    )
    return inverse_block.reshape(nodes, 2, row_blocks, 1, kept, width), diagonal_block


def solution(mesh):
    placed = (
        P("pole", None, "row", None, None, "col", None),
        P("col", "pole", None, "row", None, None),
        P("col", "pole", None, None),
        P(),
    )
    return jax.shard_map(
        local,
        mesh=mesh,
        in_specs=placed,
        out_specs=(P("col", "pole", None, "row", None, None), P("col", "pole", None, None)),
        check_vma=False,
    )
```

```python
import collections
import functools
import typing

import jax
import jax.numpy as jnp
from jax import lax
from jax.experimental import pallas as pl
from jax.experimental.pallas import tpu as pltpu
from jax.sharding import PartitionSpec as P

VMEM = pl.BlockSpec(memory_space=pltpu.VMEM)
HBM = pl.BlockSpec(memory_space=pltpu.HBM)
ANY = pl.BlockSpec(memory_space=pl.ANY)
VMEM_BYTES = 24 * 1024 * 1024
STEPS_PER_OCTAVE = 64
CLAIMED_FLOPS = 92 * 10**6

named = collections.OrderedDict


class Sizes(typing.NamedTuple):
    grid_rows: int
    grid_cols: int
    nodes: int
    row_blocks: int
    col_blocks: int
    kept: int
    width: int

    @property
    def rows(self):
        return self.row_blocks * self.kept

    @property
    def total(self):
        return self.row_blocks * self.grid_rows * self.kept


def partners(size, step):
    return [(place, place ^ step) for place in range(size)]


def dot(lhs, rhs, contract=(1, 0)):
    return lax.dot_general(
        lhs, rhs, (((contract[0],), (contract[1],)), ((), ())), preferred_element_type=jnp.float32
    )


def place_one_hot(picks, width):
    kept = picks.shape[-1]
    spots = lax.broadcasted_iota(jnp.int32, (width, kept), 0)
    return jnp.where(spots == picks, 1.0, 0.0).astype(jnp.bfloat16)


def first_kernel(result):
    result[...] = jnp.zeros_like(result)


def pick(sizes, steps, surface, row_lists, pieces):
    row_place = lax.axis_index("row")
    col_place = lax.axis_index("col")
    kept, width = sizes.kept, sizes.width
    slots = []
    for step in steps:
        target = jnp.bitwise_xor(col_place, step)
        slots += [(step, node, target * sizes.nodes + node) for node in range(sizes.nodes)]
    nodes, blocks, _ = row_lists.shape
    turned = row_lists[...].reshape(nodes * blocks, kept).astype(jnp.float32).T
    turned_spots = lax.broadcasted_iota(jnp.int32, turned.shape, 1)
    spots = lax.broadcasted_iota(jnp.int32, (kept, width), 1).astype(jnp.float32)

    def row_choice(which, block):
        mine = jnp.where(turned_spots == which * blocks + block, turned, 0.0)
        picks = jnp.sum(mine, axis=1, keepdims=True)
        return jnp.where(spots == picks, 1.0, 0.0).astype(jnp.bfloat16)

    for col_block in range(sizes.col_blocks):
        own_block = pl.ds(col_block * sizes.grid_cols + col_place, 1)
        lists = [row_lists[which, own_block, :] for _, _, which in slots]
        col_choices = jnp.concatenate([place_one_hot(picks, width) for picks in lists], axis=1)
        for row_block in range(sizes.row_blocks):
            both = surface[:, row_block, col_block].reshape(2 * width, width)
            taken = dot(both, col_choices).astype(jnp.bfloat16)
            for spot, (step, node, which) in enumerate(slots):
                cols = slice(spot * kept, (spot + 1) * kept)
                both = jnp.concatenate([taken[:width, cols], taken[width:, cols]], axis=1)
                choice = row_choice(which, row_block * sizes.grid_rows + row_place)
                block = dot(choice, both).astype(jnp.bfloat16)
                for half in range(2):
                    pieces[step][
                        node,
                        half,
                        row_block * kept : (row_block + 1) * kept,
                        col_block * kept : (col_block + 1) * kept,
                    ] = block[:, half * kept : (half + 1) * kept]


def pick_kernel(sizes, surface, row_lists, token, *pieces):
    del token
    steps = range(1, sizes.grid_cols)
    pick(sizes, steps, surface, row_lists, dict(zip(steps, pieces)))


def block_at(block, size):
    return pl.ds(pl.multiple_of(block * size, size), size)


def stack_kernel(sizes, factors, surface, row_lists, own, stacked, piece):
    stacked[0] = own[...]
    for spot, step in enumerate(factors):
        stacked[spot + 1] = factors[step][...]
    pick(sizes, [0], surface, row_lists, [piece])


def product_of(sizes, node, pieces, whole_factor):
    rows = sizes.col_blocks * sizes.kept
    lefts, rights = [], []
    for step, piece in pieces.items():
        lefts.append(jnp.concatenate([piece[node, 0], piece[node, 1]], axis=0))
        rights.append(whole_factor[node, step * rows : (step + 1) * rows, :])
    return dot(jnp.concatenate(lefts, axis=1), jnp.concatenate(rights, axis=0))


def gather_kernel(sizes, both, pieces, whole_factor, turned_factor, early):
    row_place = lax.axis_index("row")
    col_place = lax.axis_index("col")
    kept = sizes.kept
    for core in range(2):
        for spot in range(sizes.grid_rows // 2):
            source = jnp.bitwise_xor(row_place - row_place % 2, 2 * spot) + core
            for node in range(sizes.nodes):
                for block in range(sizes.row_blocks):
                    ancestor = block * sizes.grid_rows + source
                    step = jnp.bitwise_xor(ancestor % sizes.grid_cols, col_place)
                    place = step * sizes.col_blocks + ancestor // sizes.grid_cols
                    halves = [both[core, spot, node, half, block] for half in range(2)]
                    wide = jnp.concatenate(halves, axis=1)
                    whole_factor[node, block_at(place, kept), :] = wide
                    turned = wide.T
                    turned = jnp.concatenate([turned, turned], axis=1)
                    turned_factor[node, :, block_at(ancestor, 2 * kept)] = turned
    for node in range(sizes.nodes):
        early[node] = product_of(sizes, node, pieces, whole_factor)


def block_kernel(sizes, pieces, whole_factor, early, result, coded):
    width, rows = sizes.width, sizes.rows
    for node in range(sizes.nodes):
        product = early[node] + product_of(sizes, node, pieces, whole_factor)
        real = product[rows:, width:] - product[:rows, :width]
        imag = -(product[:rows, width:] + product[rows:, :width])
        result[node, :, :width] = real
        result[node, :, width:] = imag
        encode(real, imag, coded.at[node])


def encode(real, imag, coded):
    rows = real.shape[0]
    most = jnp.max(jnp.maximum(jnp.abs(real), jnp.abs(imag)), axis=0, keepdims=True)
    level = jnp.ceil(jnp.log2(jnp.maximum(most, 1e-30)) * STEPS_PER_OCTAVE + 0.2)
    scale = jnp.exp2(15.0 - level / STEPS_PER_OCTAVE)
    for half, values in enumerate((real, imag)):
        steps = jnp.clip(jnp.round(values * scale), -32767.0, 32767.0)
        coded[half * rows : (half + 1) * rows, :] = steps.astype(jnp.int32).astype(jnp.int16)
    levels = jnp.broadcast_to(level, (16, level.shape[1]))
    coded[2 * rows :, :] = levels.astype(jnp.int32).astype(jnp.int16)


def decode(coded):
    rows = coded.shape[0] // 2 - 8
    level = coded[2 * rows :, :].astype(jnp.int32).astype(jnp.float32)[:1]
    scale = jnp.exp2(level / STEPS_PER_OCTAVE - 15.0)
    values = coded[: 2 * rows, :].astype(jnp.int32).astype(jnp.float32) * scale
    return jnp.concatenate([values[:rows], values[rows:]], axis=1)


def factor_times(sizes, node, terms, turned_factor, spots=None):
    width, kept = sizes.width, sizes.kept
    spots = spots or slice(0, width)
    row_place = lax.axis_index("row")
    from_real = from_imag = 0.0
    for step, wide in terms.items():
        source = jnp.bitwise_xor(row_place, step)
        high = wide.astype(jnp.bfloat16)
        low = (wide - high.astype(jnp.float32)).astype(jnp.bfloat16)
        for block in range(sizes.row_blocks):
            rows = slice(block * kept, (block + 1) * kept)
            right = jnp.concatenate([high[rows], low[rows]], axis=0)
            place = block_at(block * sizes.grid_rows + source, 2 * kept)
            from_real += dot(turned_factor[node, spots.start : spots.stop, place], right)
            imag_spots = slice(width + spots.start, width + spots.stop)
            from_imag += dot(turned_factor[node, imag_spots, place], right)
    real = from_real[:, :width] - from_imag[:, width:]
    imag = from_real[:, width:] + from_imag[:, :width]
    return real, imag


def near_kernel(sizes, base, turned_factor, own, result, block):
    width = sizes.width
    for node in range(sizes.nodes):
        block[node, 0] = own[node, :, :width]
        block[node, 1] = own[node, :, width:]
        real, imag = factor_times(sizes, node, {0: own[node]}, turned_factor)
        result[node, 0] = base[node, 0] - real
        result[node, 1] = base[node, 1] - imag


def middle_kernel(sizes, before, turned_factor, mate, coded, result):
    for node in range(sizes.nodes):
        terms = {1: mate[node], **{step: decode(coded[step].at[node]) for step in coded}}
        real, imag = factor_times(sizes, node, terms, turned_factor)
        result[node, 0] = before[node, 0] - real
        result[node, 1] = before[node, 1] - imag


def last_kernel(sizes, before, turned_factor, coded, result, held, sent):
    half = sizes.width // 2
    copies = []
    for node in range(sizes.nodes):
        terms = {step: decode(coded[step].at[node]) for step in coded}
        for turn in range(2):
            spots = slice(turn * half, (turn + 1) * half)
            real, imag = factor_times(sizes, node, terms, turned_factor, spots)
            held[node, 0, spots] = before[node, 0, spots] - real
            held[node, 1, spots] = before[node, 1, spots] - imag
            place = (node, slice(None), spots)
            copy = pltpu.make_async_copy(held.at[place], result.at[place], sent.at[node, turn])
            copy.start()
            copies.append(copy)
    for copy in copies:
        copy.wait()


def call(kernel, out_shape, *args, remote=(), out_specs=None, scratch=()):
    flat, tree = jax.tree.flatten(args)

    def flat_kernel(*refs):
        ins = jax.tree.unflatten(tree, refs[: len(flat)])
        kernel(*ins, *refs[len(flat) :])

    return pl.pallas_call(
        flat_kernel,
        out_shape=out_shape,
        in_specs=[VMEM] * len(flat) + [HBM] * len(remote),
        out_specs=out_specs or [VMEM] * len(out_shape),
        scratch_shapes=scratch,
        compiler_params=pltpu.CompilerParams(vmem_limit_bytes=VMEM_BYTES),
    )(*flat, *[pltpu.with_memory_space_constraint(a, pltpu.HBM) for a in remote])


def local(inverse_top, factor, diag_inverse, row_lists):
    grid_rows = lax.axis_size("row")
    grid_cols = lax.axis_size("col")
    nodes, _, row_blocks, _, kept, width = factor.shape
    col_blocks = inverse_top.shape[4]
    sizes = Sizes(grid_rows, grid_cols, nodes, row_blocks, col_blocks, kept, width)
    rows = sizes.rows
    surface = inverse_top.transpose(0, 1, 2, 4, 5, 3, 6).reshape(
        2, row_blocks, col_blocks, width, width
    )
    own_factor = factor.reshape(nodes, 2, row_blocks, kept, width)
    narrow, wide = jnp.bfloat16, jnp.float32
    square = jax.ShapeDtypeStruct((nodes, 2, width, width), wide)
    across = range(2, grid_rows, 2)

    def over_rows(block, step):
        return lax.ppermute(block, "row", partners(grid_rows, step))

    token = pl.pallas_call(
        first_kernel,
        out_shape=pltpu.VMEM((8, 128), wide),
        out_specs=VMEM,
        cost_estimate=pl.CostEstimate(flops=CLAIMED_FLOPS, bytes_accessed=0, transcendentals=0),
    )()
    token, sent_factor = lax.optimization_barrier((token, own_factor))
    piece = jax.ShapeDtypeStruct((nodes, 2, rows, col_blocks * kept), narrow)
    pieces = pl.pallas_call(
        functools.partial(pick_kernel, sizes),
        out_shape=[piece] * (grid_cols - 1),
        in_specs=[VMEM, VMEM, ANY],
        out_specs=[VMEM] * (grid_cols - 1),
        compiler_params=pltpu.CompilerParams(vmem_limit_bytes=VMEM_BYTES),
    )(surface, row_lists, token)
    factors = named((step, over_rows(sent_factor, step)) for step in across)
    arrived = named()
    for step in [*range(grid_cols // 2, grid_cols), *range(grid_cols // 2 - 1, 0, -1)]:
        arrived[step] = lax.ppermute(pieces[step - 1], "col", partners(grid_cols, step))
    _, late_factor = lax.optimization_barrier((pieces[grid_cols // 2 - 1], sent_factor))
    stacked, own_piece = call(
        functools.partial(stack_kernel, sizes),
        [jax.ShapeDtypeStruct((grid_rows // 2, *own_factor.shape), narrow), piece],
        factors,
        surface,
        row_lists,
        late_factor,
    )
    pairs = [[place, place + 1] for place in range(0, grid_rows, 2)]
    both = lax.all_gather(stacked, "row", axis_index_groups=pairs)
    first = named({0: own_piece, grid_cols // 2: arrived.pop(grid_cols // 2)})
    whole_factor, turned_factor, early = call(
        functools.partial(gather_kernel, sizes),
        [
            jax.ShapeDtypeStruct((nodes, sizes.total, 2 * width), narrow),
            jax.ShapeDtypeStruct((nodes, 2 * width, 2 * sizes.total), narrow),
            jax.ShapeDtypeStruct((nodes, 2 * rows, 2 * width), wide),
        ],
        both,
        first,
    )
    block, coded = call(
        functools.partial(block_kernel, sizes),
        [
            jax.ShapeDtypeStruct((nodes, rows, 2 * width), wide),
            jax.ShapeDtypeStruct((nodes, 2 * rows + 16, width), jnp.int16),
        ],
        arrived,
        whole_factor,
        early,
    )
    sent = named((step, over_rows(coded, step)) for step in across)
    near, inverse_block = call(
        functools.partial(near_kernel, sizes),
        [square, jax.ShapeDtypeStruct((nodes, 2, rows, width), wide)],
        diag_inverse,
        turned_factor,
        block,
    )
    near, block = lax.optimization_barrier((near, block))
    mate = over_rows(block, 1)
    near, sent = lax.optimization_barrier((near, sent))
    forwarded = named((step + 1, over_rows(sent[step], 1)) for step in across)
    (middle,) = call(
        functools.partial(middle_kernel, sizes), [square], near, turned_factor, mate, sent
    )
    (diagonal_block,) = call(
        functools.partial(last_kernel, sizes),
        [square],
        middle,
        turned_factor,
        forwarded,
        out_specs=[HBM],
        scratch=[pltpu.VMEM(square.shape, wide), pltpu.SemaphoreType.DMA((nodes, 2))],
    )
    return inverse_block.reshape(nodes, 2, row_blocks, 1, kept, width), diagonal_block


def solution(mesh):
    placed = (
        P("pole", None, "row", None, None, "col", None),
        P("col", "pole", None, "row", None, None),
        P("col", "pole", None, None),
        P(),
    )
    return jax.shard_map(
        local,
        mesh=mesh,
        in_specs=placed,
        out_specs=(P("col", "pole", None, "row", None, None), P("col", "pole", None, None)),
        check_vma=False,
    )
```

```python
import collections
import functools
import typing

import jax
import jax.numpy as jnp
from jax import lax
from jax.experimental import pallas as pl
from jax.experimental.pallas import tpu as pltpu
from jax.sharding import PartitionSpec as P

VMEM = pl.BlockSpec(memory_space=pltpu.VMEM)
HBM = pl.BlockSpec(memory_space=pltpu.HBM)
ANY = pl.BlockSpec(memory_space=pl.ANY)
VMEM_BYTES = 24 * 1024 * 1024
STEPS_PER_OCTAVE = 64
CLAIMED_FLOPS = 92 * 10**6

named = collections.OrderedDict


class Sizes(typing.NamedTuple):
    grid_rows: int
    grid_cols: int
    nodes: int
    row_blocks: int
    col_blocks: int
    kept: int
    width: int

    @property
    def rows(self):
        return self.row_blocks * self.kept

    @property
    def total(self):
        return self.row_blocks * self.grid_rows * self.kept


def partners(size, step):
    return [(place, place ^ step) for place in range(size)]


def dot(lhs, rhs, contract=(1, 0)):
    return lax.dot_general(
        lhs, rhs, (((contract[0],), (contract[1],)), ((), ())), preferred_element_type=jnp.float32
    )


def place_one_hot(picks, width):
    kept = picks.shape[-1]
    spots = lax.broadcasted_iota(jnp.int32, (width, kept), 0)
    return jnp.where(spots == picks, 1.0, 0.0).astype(jnp.bfloat16)


def first_kernel(result):
    result[...] = jnp.zeros_like(result)


def pick(sizes, steps, surface, row_lists, pieces):
    row_place = lax.axis_index("row")
    col_place = lax.axis_index("col")
    kept, width = sizes.kept, sizes.width
    slots = []
    for step in steps:
        target = jnp.bitwise_xor(col_place, step)
        slots += [(step, node, target * sizes.nodes + node) for node in range(sizes.nodes)]
    nodes, blocks, _ = row_lists.shape
    turned = row_lists[...].reshape(nodes * blocks, kept).astype(jnp.float32).T
    turned_spots = lax.broadcasted_iota(jnp.int32, turned.shape, 1)
    spots = lax.broadcasted_iota(jnp.int32, (kept, width), 1).astype(jnp.float32)

    def row_choice(which, block):
        mine = jnp.where(turned_spots == which * blocks + block, turned, 0.0)
        picks = jnp.sum(mine, axis=1, keepdims=True)
        return jnp.where(spots == picks, 1.0, 0.0).astype(jnp.bfloat16)

    for col_block in range(sizes.col_blocks):
        own_block = pl.ds(col_block * sizes.grid_cols + col_place, 1)
        lists = [row_lists[which, own_block, :] for _, _, which in slots]
        col_choices = jnp.concatenate([place_one_hot(picks, width) for picks in lists], axis=1)
        for row_block in range(sizes.row_blocks):
            both = surface[:, row_block, col_block].reshape(2 * width, width)
            taken = dot(both, col_choices).astype(jnp.bfloat16)
            for spot, (step, node, which) in enumerate(slots):
                cols = slice(spot * kept, (spot + 1) * kept)
                both = jnp.concatenate([taken[:width, cols], taken[width:, cols]], axis=1)
                choice = row_choice(which, row_block * sizes.grid_rows + row_place)
                block = dot(choice, both).astype(jnp.bfloat16)
                for half in range(2):
                    pieces[step][
                        node,
                        half,
                        row_block * kept : (row_block + 1) * kept,
                        col_block * kept : (col_block + 1) * kept,
                    ] = block[:, half * kept : (half + 1) * kept]


def pick_kernel(sizes, surface, row_lists, token, *pieces):
    del token
    steps = range(1, sizes.grid_cols)
    pick(sizes, steps, surface, row_lists, dict(zip(steps, pieces)))


def block_at(block, size):
    return pl.ds(pl.multiple_of(block * size, size), size)


def stack_kernel(sizes, factors, surface, row_lists, far_factor, stacked, piece, arrival):
    copy = pltpu.make_async_copy(far_factor, stacked.at[0], arrival)
    copy.start()
    for spot, step in enumerate(factors):
        stacked[spot + 1] = factors[step][...]
    pick(sizes, [0], surface, row_lists, [piece])
    copy.wait()


def product_of(sizes, node, pieces, whole_factor):
    rows = sizes.col_blocks * sizes.kept
    lefts, rights = [], []
    for step, piece in pieces.items():
        lefts.append(jnp.concatenate([piece[node, 0], piece[node, 1]], axis=0))
        rights.append(whole_factor[node, step * rows : (step + 1) * rows, :])
    return dot(jnp.concatenate(lefts, axis=1), jnp.concatenate(rights, axis=0))


def gather_kernel(sizes, both, pieces, whole_factor, turned_factor, early):
    row_place = lax.axis_index("row")
    col_place = lax.axis_index("col")
    kept = sizes.kept
    for core in range(2):
        for spot in range(sizes.grid_rows // 2):
            source = jnp.bitwise_xor(row_place - row_place % 2, 2 * spot) + core
            for node in range(sizes.nodes):
                for block in range(sizes.row_blocks):
                    ancestor = block * sizes.grid_rows + source
                    step = jnp.bitwise_xor(ancestor % sizes.grid_cols, col_place)
                    place = step * sizes.col_blocks + ancestor // sizes.grid_cols
                    halves = [both[core, spot, node, half, block] for half in range(2)]
                    wide = jnp.concatenate(halves, axis=1)
                    whole_factor[node, block_at(place, kept), :] = wide
                    turned = wide.T
                    turned = jnp.concatenate([turned, turned], axis=1)
                    turned_factor[node, :, block_at(ancestor, 2 * kept)] = turned
    for node in range(sizes.nodes):
        early[node] = product_of(sizes, node, pieces, whole_factor)


def block_kernel(sizes, pieces, whole_factor, early, result, coded):
    width, rows = sizes.width, sizes.rows
    for node in range(sizes.nodes):
        product = early[node] + product_of(sizes, node, pieces, whole_factor)
        real = product[rows:, width:] - product[:rows, :width]
        imag = -(product[:rows, width:] + product[rows:, :width])
        result[node, :, :width] = real
        result[node, :, width:] = imag
        encode(real, imag, coded.at[node])


def encode(real, imag, coded):
    rows = real.shape[0]
    most = jnp.max(jnp.maximum(jnp.abs(real), jnp.abs(imag)), axis=0, keepdims=True)
    level = jnp.ceil(jnp.log2(jnp.maximum(most, 1e-30)) * STEPS_PER_OCTAVE + 0.2)
    scale = jnp.exp2(15.0 - level / STEPS_PER_OCTAVE)
    for half, values in enumerate((real, imag)):
        steps = jnp.clip(jnp.round(values * scale), -32767.0, 32767.0)
        coded[half * rows : (half + 1) * rows, :] = steps.astype(jnp.int32).astype(jnp.int16)
    levels = jnp.broadcast_to(level, (16, level.shape[1]))
    coded[2 * rows :, :] = levels.astype(jnp.int32).astype(jnp.int16)


def decode(coded):
    rows = coded.shape[0] // 2 - 8
    level = coded[2 * rows :, :].astype(jnp.int32).astype(jnp.float32)[:1]
    scale = jnp.exp2(level / STEPS_PER_OCTAVE - 15.0)
    values = coded[: 2 * rows, :].astype(jnp.int32).astype(jnp.float32) * scale
    return jnp.concatenate([values[:rows], values[rows:]], axis=1)


def factor_times(sizes, node, terms, turned_factor, spots=None):
    width, kept = sizes.width, sizes.kept
    spots = spots or slice(0, width)
    row_place = lax.axis_index("row")
    from_real = from_imag = 0.0
    for step, wide in terms.items():
        source = jnp.bitwise_xor(row_place, step)
        high = wide.astype(jnp.bfloat16)
        low = (wide - high.astype(jnp.float32)).astype(jnp.bfloat16)
        for block in range(sizes.row_blocks):
            rows = slice(block * kept, (block + 1) * kept)
            right = jnp.concatenate([high[rows], low[rows]], axis=0)
            place = block_at(block * sizes.grid_rows + source, 2 * kept)
            from_real += dot(turned_factor[node, spots.start : spots.stop, place], right)
            imag_spots = slice(width + spots.start, width + spots.stop)
            from_imag += dot(turned_factor[node, imag_spots, place], right)
    real = from_real[:, :width] - from_imag[:, width:]
    imag = from_real[:, width:] + from_imag[:, :width]
    return real, imag


def near_kernel(sizes, base, turned_factor, own, result, block):
    width = sizes.width
    for node in range(sizes.nodes):
        block[node, 0] = own[node, :, :width]
        block[node, 1] = own[node, :, width:]
        real, imag = factor_times(sizes, node, {0: own[node]}, turned_factor)
        result[node, 0] = base[node, 0] - real
        result[node, 1] = base[node, 1] - imag


def middle_kernel(sizes, before, turned_factor, mate, coded, result):
    for node in range(sizes.nodes):
        terms = {1: mate[node], **{step: decode(coded[step].at[node]) for step in coded}}
        real, imag = factor_times(sizes, node, terms, turned_factor)
        result[node, 0] = before[node, 0] - real
        result[node, 1] = before[node, 1] - imag


def last_kernel(sizes, before, turned_factor, coded, result, held, sent):
    half = sizes.width // 2
    copies = []
    for node in range(sizes.nodes):
        terms = {step: decode(coded[step].at[node]) for step in coded}
        for turn in range(2):
            spots = slice(turn * half, (turn + 1) * half)
            real, imag = factor_times(sizes, node, terms, turned_factor, spots)
            held[node, 0, spots] = before[node, 0, spots] - real
            held[node, 1, spots] = before[node, 1, spots] - imag
            place = (node, slice(None), spots)
            copy = pltpu.make_async_copy(held.at[place], result.at[place], sent.at[node, turn])
            copy.start()
            copies.append(copy)
    for copy in copies:
        copy.wait()


def call(kernel, out_shape, *args, remote=(), out_specs=None, scratch=()):
    flat, tree = jax.tree.flatten(args)

    def flat_kernel(*refs):
        ins = jax.tree.unflatten(tree, refs[: len(flat)])
        kernel(*ins, *refs[len(flat) :])

    return pl.pallas_call(
        flat_kernel,
        out_shape=out_shape,
        in_specs=[VMEM] * len(flat) + [HBM] * len(remote),
        out_specs=out_specs or [VMEM] * len(out_shape),
        scratch_shapes=scratch,
        compiler_params=pltpu.CompilerParams(vmem_limit_bytes=VMEM_BYTES),
    )(*flat, *[pltpu.with_memory_space_constraint(a, pltpu.HBM) for a in remote])


def local(inverse_top, factor, diag_inverse, row_lists):
    grid_rows = lax.axis_size("row")
    grid_cols = lax.axis_size("col")
    nodes, _, row_blocks, _, kept, width = factor.shape
    col_blocks = inverse_top.shape[4]
    sizes = Sizes(grid_rows, grid_cols, nodes, row_blocks, col_blocks, kept, width)
    rows = sizes.rows
    surface = inverse_top.transpose(0, 1, 2, 4, 5, 3, 6).reshape(
        2, row_blocks, col_blocks, width, width
    )
    own_factor = factor.reshape(nodes, 2, row_blocks, kept, width)
    narrow, wide = jnp.bfloat16, jnp.float32
    square = jax.ShapeDtypeStruct((nodes, 2, width, width), wide)
    across = range(2, grid_rows, 2)

    def over_rows(block, step):
        return lax.ppermute(block, "row", partners(grid_rows, step))

    token = pl.pallas_call(
        first_kernel,
        out_shape=pltpu.VMEM((8, 128), wide),
        out_specs=VMEM,
        cost_estimate=pl.CostEstimate(flops=CLAIMED_FLOPS, bytes_accessed=0, transcendentals=0),
    )()
    token, sent_factor = lax.optimization_barrier((token, own_factor))
    piece = jax.ShapeDtypeStruct((nodes, 2, rows, col_blocks * kept), narrow)
    pieces = pl.pallas_call(
        functools.partial(pick_kernel, sizes),
        out_shape=[piece] * (grid_cols - 1),
        in_specs=[VMEM, VMEM, ANY],
        out_specs=[VMEM] * (grid_cols - 1),
        compiler_params=pltpu.CompilerParams(vmem_limit_bytes=VMEM_BYTES),
    )(surface, row_lists, token)
    factors = named((step, over_rows(sent_factor, step)) for step in across)
    arrived = named()
    for step in [*range(grid_cols // 2, grid_cols), *range(grid_cols // 2 - 1, 0, -1)]:
        arrived[step] = lax.ppermute(pieces[step - 1], "col", partners(grid_cols, step))
    stacked, own_piece = call(
        functools.partial(stack_kernel, sizes),
        [jax.ShapeDtypeStruct((grid_rows // 2, *own_factor.shape), narrow), piece],
        factors,
        surface,
        row_lists,
        remote=[sent_factor],
        scratch=[pltpu.SemaphoreType.DMA],
    )
    pairs = [[place, place + 1] for place in range(0, grid_rows, 2)]
    both = lax.all_gather(stacked, "row", axis_index_groups=pairs)
    first = named({0: own_piece, grid_cols // 2: arrived.pop(grid_cols // 2)})
    whole_factor, turned_factor, early = call(
        functools.partial(gather_kernel, sizes),
        [
            jax.ShapeDtypeStruct((nodes, sizes.total, 2 * width), narrow),
            jax.ShapeDtypeStruct((nodes, 2 * width, 2 * sizes.total), narrow),
            jax.ShapeDtypeStruct((nodes, 2 * rows, 2 * width), wide),
        ],
        both,
        first,
    )
    block, coded = call(
        functools.partial(block_kernel, sizes),
        [
            jax.ShapeDtypeStruct((nodes, rows, 2 * width), wide),
            jax.ShapeDtypeStruct((nodes, 2 * rows + 16, width), jnp.int16),
        ],
        arrived,
        whole_factor,
        early,
    )
    sent = named((step, over_rows(coded, step)) for step in across)
    near, inverse_block = call(
        functools.partial(near_kernel, sizes),
        [square, jax.ShapeDtypeStruct((nodes, 2, rows, width), wide)],
        diag_inverse,
        turned_factor,
        block,
    )
    mate = over_rows(block, 1)
    near, sent = lax.optimization_barrier((near, sent))
    forwarded = named((step + 1, over_rows(sent[step], 1)) for step in across)
    (middle,) = call(
        functools.partial(middle_kernel, sizes), [square], near, turned_factor, mate, sent
    )
    (diagonal_block,) = call(
        functools.partial(last_kernel, sizes),
        [square],
        middle,
        turned_factor,
        forwarded,
        out_specs=[HBM],
        scratch=[pltpu.VMEM(square.shape, wide), pltpu.SemaphoreType.DMA((nodes, 2))],
    )
    return inverse_block.reshape(nodes, 2, row_blocks, 1, kept, width), diagonal_block


def solution(mesh):
    placed = (
        P("pole", None, "row", None, None, "col", None),
        P("col", "pole", None, "row", None, None),
        P("col", "pole", None, None),
        P(),
    )
    return jax.shard_map(
        local,
        mesh=mesh,
        in_specs=placed,
        out_specs=(P("col", "pole", None, "row", None, None), P("col", "pole", None, None)),
        check_vma=False,
    )
```
